128 devices in a mesh: dp: 16 (over y, x), tensor: 8 (over z, core).
Axes of the slice: x: 4, y: 4, z: 4, core: 2. Of those that a mesh axis runs over, the one named last changes fastest.
Arguments:
- pre_norm: bfloat16 [4096, 4096], P(('dp', 'tensor')), may hold values from -140 to 140
- out_grad: bfloat16 [4096, 4096], P(('dp', 'tensor')), may hold values from -6 to 6
- routes: int32 [4096, 8], P(('dp', 'tensor')), may hold values from 0 to 63, all different within a row; in each aligned block of 32 rows (0 to 31, 32 to 63, ...) at most 6 rows name the same one
- gate_probs: float32 [4096, 8], P(('dp', 'tensor')), may hold values from 0 to 1, as said below
- norm_gain: float32 [4096], replicated, may hold values from 0.5 to 1.5
- router_weight: bfloat16 [4096, 64], replicated, may hold values from -0.09375 to 0.09375
- w_gate: bfloat16 [128, 4096, 768], P(('dp', 'tensor')), may hold values from -0.09375 to 0.09375
- w_up: bfloat16 [128, 4096, 768], P(('dp', 'tensor')), may hold values from -0.09375 to 0.09375
- w_down: bfloat16 [128, 768, 4096], P(('dp', 'tensor')), may hold values from -0.15625 to 0.15625
- context: bfloat16 [4096, 8192], P('dp', 'tensor'), may hold values from -6 to 6
- out_weight: bfloat16 [4096, 8192], P('dp', 'tensor'), may hold values from -0.0625 to 0.0625
Outputs:
- residual_grad: bfloat16 [4096, 4096], P(('dp', 'tensor'))
- gate_grad: float32 [4096, 8], P(('dp', 'tensor'))
- router_grad: float32 [4096, 64], P('tensor')
- gain_grad: float32 [4096], P('tensor')
- context_grad: bfloat16 [4096, 8192], P('dp', 'tensor')
- weight_grad: bfloat16 [4096, 8192], P('dp', 'tensor')
The draws below stay inside these ranges and needn't reach their ends.
Inputs may be any that keep to these rules, and one draw needn't show every extreme that they name: `routes`: each row names 8 different experts; among the 32 tokens of one device (aligned blocks) no expert is named more than 6 times, a bound that some block reaches. `gate_probs`: each row is positive and sums to one.
All inputs are finite; a program needn't handle non-finite values.
Results may differ from the reference program's by a relative error of at most 0.019.
Values may be sent and summed in bfloat16 or wider, within the bound.
No kernel may reach another device: no remote copies, remote signals or barrier semaphores. Data moves between devices by JAX's collectives and lax.ppermute only.
A program may use at most 192 MiB of HBM per device.

```python
import math
import jax
import jax.numpy as jnp
import numpy as np
from jax import lax

D = 4096
FF = 1536
TOPK = 8
ETP = 2
TOK_DEV = 32
EXPERTS = 64
CAP = 6
TOKENS = 4096
HQ = 8192
N_DP = 16


def draw_pre_norm(key, part):
    key = jax.random.fold_in(key, 11)
    base_key, row_key, col_key = jax.random.split(key, 3)
    row_scale = jnp.exp(jax.random.uniform(row_key, (TOKENS, 1), jnp.float32) * math.log(10.0))
    col_scale = jnp.exp(jax.random.uniform(col_key, (1, D), jnp.float32) * math.log(10.0))
    base = jax.random.truncated_normal(base_key, -4.0, 4.0, (TOKENS, D), jnp.float32)
    return (base * row_scale * col_scale / 3.0).astype(jnp.bfloat16)


def draw_gate_probs(key, part):
    key = jax.random.fold_in(key, 23)
    logits = jax.random.normal(key, (TOKENS, TOPK), jnp.float32) * 1.5
    return jax.nn.softmax(logits, axis=-1).astype(jnp.float32)


def shard_levels(own_key, extent, pieces, low, largest):
    factor_of, own = 1.0, jax.random.fold_in(own_key, 6)
    for axis_at, parts in pieces:
        draws = jnp.exp(jax.random.uniform(jax.random.fold_in(own, axis_at), (parts,), jnp.float32, low / len(pieces), largest / len(pieces)))
        factor_of = factor_of * jnp.repeat(draws, extent[axis_at] // parts).reshape([-1 if axis == axis_at else 1 for axis in range(len(extent))])
    return factor_of


def shared_out(stream_key, own, number, rows, amount, top, reach, skew):
    sequence = jax.random.permutation(stream_key, amount)
    crowded, ordinary = portions_of(amount, rows * top, reach, skew, True), portions_of(amount, rows * top, reach, skew, False)
    places = jnp.arange(amount)

    def named(tallies, turn):
        used = int((tallies > 0).sum())
        fixed = max(1, used // 4)
        passed = fixed + (places - fixed + turn * (used - fixed)) % max(1, amount - fixed)
        return jnp.zeros((amount,), jnp.int32).at[sequence[jnp.where(places < fixed, places, passed)]].set(jnp.asarray(tallies, jnp.int32))

    tallies = jnp.where(number % 4 == 0, named(crowded, number // 4), named(ordinary, number - number // 4 - 1))
    mixed = jax.random.permutation(jax.random.fold_in(own, 3), amount)
    source_of, receiver = mixed[0:amount // 2 * 2:2], mixed[1:amount // 2 * 2:2]
    margin = jnp.minimum(tallies[source_of] - 1, reach - tallies[receiver]) // 2
    margin = jnp.where((source_of == sequence[0]) | (receiver == sequence[0]) | (tallies[receiver] == 0), 0, jnp.maximum(margin, 0))
    passed = jax.random.randint(jax.random.fold_in(own, 4), (amount // 2,), 0, 1 << 20) % (margin + 1)
    tallies = tallies.at[source_of].add(-passed).at[receiver].add(passed)
    items = jnp.searchsorted(jnp.cumsum(tallies), jnp.arange(rows * top), side="right").astype(jnp.int32)
    grid = items.reshape(top, rows).T
    grid = grid[jax.random.permutation(jax.random.fold_in(own, 1), rows)]
    turn = jax.random.randint(jax.random.fold_in(own, 2), (rows, 1), 0, top)
    return jnp.take_along_axis(grid, (jnp.arange(top)[None, :] + turn) % top, axis=1)


def portions_of(count, total, bound, skew, full):
    loads = [(1 << 20) // math.isqrt(rank ** skew) + 1 for rank in range(1, count + 1)]
    largest = bound if full else min(bound, max(-(-total // count), total * loads[0] // sum(loads)))
    least = 1 if total - largest >= count - 1 else 0
    counts, rest = [largest] + [least] * (count - 1), total - largest - least * (count - 1)
    while rest > 0:
        movable = [i for i in range(1, count) if counts[i] < largest] or [i for i in range(1, count) if counts[i] < bound]
        pool, budget = sum([loads[i] for i in movable]), rest
        for i in movable:
            more = min(bound - counts[i], max(1, budget * loads[i] // pool), rest)
            counts[i] = counts[i] + more
            rest = rest - more
    return np.array(counts)


def scatter_about(stream_key, extent, spread, limit, cuts=(), kind=jnp.bfloat16):
    drawn = jax.random.normal(stream_key, extent, jnp.float32) * spread
    if len(cuts) > 0:
        drawn = shard_levels(stream_key, extent, cuts, -0.22, 0.18) * drawn
    return jnp.clip(drawn, min=-limit, max=limit).astype(kind)


def setup_inputs(seed: int = 0) -> dict:
    seeds = jax.random.split(jax.random.key(seed), 12)
    pre_norm = draw_pre_norm(jax.random.fold_in(seeds[11], 71), 0)
    out_grad = scatter_about(seeds[1], (TOKENS, D), 1.0, 6.0, ((0, 128),))
    routes_keys = jax.random.split(jax.random.fold_in(seeds[2], 1), TOKENS // TOK_DEV)
    routes_turns = jax.random.permutation(jax.random.fold_in(seeds[2], 3), TOKENS // TOK_DEV)
    routes = jax.vmap(lambda own, number: shared_out(jax.random.fold_in(seeds[2], 2), own, number, TOK_DEV, EXPERTS, TOPK, CAP, 2))(routes_keys, routes_turns).reshape((TOKENS, TOPK))
    gate_probs = draw_gate_probs(jax.random.fold_in(seeds[11], 71), 0)
    norm_gain = jnp.clip(1.0 + 0.1 * jax.random.normal(seeds[4], (D,), jnp.float32), 0.5, 1.5)
    router_weight = scatter_about(seeds[5], (D, EXPERTS), D ** -0.5, 0.09375)
    w_gate = scatter_about(seeds[6], (EXPERTS * ETP, D, FF // ETP), D ** -0.5, 0.09375, ((0, 128),))
    w_up = scatter_about(seeds[7], (EXPERTS * ETP, D, FF // ETP), D ** -0.5, 0.09375, ((0, 128),))
    w_down = scatter_about(seeds[8], (EXPERTS * ETP, FF // ETP, D), FF ** -0.5, 0.15625, ((0, 128),))
    context = scatter_about(seeds[9], (TOKENS, HQ), 1.0, 6.0, ((0, 16), (1, 8)))
    out_weight = scatter_about(seeds[10], (D, HQ), HQ ** -0.5, 0.0625, ((0, 16), (1, 8)))
    return dict(pre_norm=pre_norm, out_grad=out_grad, routes=routes, gate_probs=gate_probs, norm_gain=norm_gain, router_weight=router_weight, w_gate=w_gate, w_up=w_up, w_down=w_down, context=context, out_weight=out_weight)


def half_terms(token_rows, grad_rows, gate_mat, up_mat, down_mat):
    gate_pre = jnp.dot(token_rows, gate_mat, preferred_element_type=jnp.float32)
    up_pre = jnp.dot(token_rows, up_mat, preferred_element_type=jnp.float32)
    upstream = jnp.dot(grad_rows, down_mat.T, preferred_element_type=jnp.float32)
    gate_sig = jax.nn.sigmoid(gate_pre)
    activation = gate_pre * gate_sig * up_pre
    partial_value = lax.optimization_barrier(jnp.sum(activation * upstream, axis=-1)).astype(jnp.bfloat16)
    grad_up = (upstream * gate_pre * gate_sig).astype(jnp.bfloat16)
    grad_gate = (upstream * up_pre * gate_sig * (1.0 + gate_pre * (1.0 - gate_sig))).astype(jnp.bfloat16)
    back_rows = jnp.dot(grad_gate, gate_mat.T, preferred_element_type=jnp.float32)
    back_rows = back_rows + jnp.dot(grad_up, up_mat.T, preferred_element_type=jnp.float32)
    return (back_rows.astype(jnp.bfloat16), partial_value)

def reference(pre_norm, out_grad, routes, gate_probs, norm_gain, router_weight, w_gate, w_up, w_down, context, out_weight):
    hidden = pre_norm.astype(jnp.float32)
    inverse = lax.rsqrt(lax.optimization_barrier(jnp.mean(hidden * hidden, axis=-1, keepdims=True)) + 1e-06)
    normed = (hidden * inverse * norm_gain).astype(jnp.bfloat16)
    slot_count = TOKENS * TOPK
    flat_route = routes.reshape(slot_count)
    flat_gate = gate_probs.reshape(slot_count)
    padded_tokens = jnp.concatenate([normed, jnp.zeros((1, D), jnp.bfloat16)], axis=0)
    padded_grads = jnp.concatenate([out_grad, jnp.zeros((1, D), jnp.bfloat16)], axis=0)
    padded_gates = jnp.concatenate([flat_gate, jnp.zeros((1,), jnp.float32)], axis=0)
    most_rows = TOKENS // TOK_DEV * CAP

    def visit(carry, expert):
        accum, slot_grad = carry
        chosen = jnp.nonzero(flat_route == expert, size=most_rows, fill_value=slot_count)[0].astype(jnp.int32)
        owner = (chosen // TOPK).astype(jnp.int32)
        token_rows = padded_tokens[owner]
        grad_rows = padded_grads[owner]
        term_sum = jnp.zeros((most_rows, D), jnp.float32)
        part_sum = jnp.zeros((most_rows,), jnp.float32)
        for half in range(ETP):
            index = (expert * ETP + half).astype(jnp.int32)
            gate_mat = lax.dynamic_index_in_dim(w_gate, index, 0, keepdims=False)
            up_mat = lax.dynamic_index_in_dim(w_up, index, 0, keepdims=False)
            down_mat = lax.dynamic_index_in_dim(w_down, index, 0, keepdims=False)
            back_rows, partial_value = half_terms(token_rows, grad_rows, gate_mat, up_mat, down_mat)
            term_sum = term_sum + back_rows.astype(jnp.float32)
            part_sum = part_sum + partial_value.astype(jnp.float32)
        accum = accum.at[owner].add(padded_gates[chosen][:, None] * term_sum)
        slot_grad = slot_grad.at[chosen].add(part_sum)
        return ((accum, slot_grad), None)
    start_state = (jnp.zeros((TOKENS + 1, D), jnp.float32), jnp.zeros((slot_count + 1,), jnp.float32))
    (accum, slot_grad), unused = lax.scan(visit, start_state, jnp.arange(EXPERTS, dtype=jnp.int32))
    gate_grad = slot_grad[:slot_count].reshape(TOKENS, TOPK)
    weighted = lax.optimization_barrier(jnp.sum(gate_probs * gate_grad, axis=-1, keepdims=True))
    logit_grad = (gate_probs * (gate_grad - weighted)).astype(jnp.bfloat16)
    matches = (routes[:, :, None] == jnp.arange(EXPERTS, dtype=jnp.int32)[None, None, :]).astype(jnp.float32)
    logit_full = lax.optimization_barrier(jnp.sum(logit_grad.astype(jnp.float32)[:, :, None] * matches, axis=1)).astype(jnp.bfloat16)
    normed_grad = accum[:TOKENS] + jnp.dot(logit_full, router_weight.T, preferred_element_type=jnp.float32)
    router_grad = jnp.dot(normed.T, logit_full, preferred_element_type=jnp.float32)
    gain_grad = lax.optimization_barrier(jnp.sum(normed_grad * hidden * inverse, axis=0))
    scaled = norm_gain * normed_grad
    cubed = inverse * inverse * inverse
    residual_grad = (out_grad.astype(jnp.float32) + inverse * scaled - hidden * cubed * lax.optimization_barrier(jnp.mean(hidden * scaled, axis=-1, keepdims=True))).astype(jnp.bfloat16)
    context_grad = jnp.dot(residual_grad, out_weight, preferred_element_type=jnp.float32).astype(jnp.bfloat16)
    grouped_grads = residual_grad.reshape(N_DP, TOKENS // N_DP, D)
    grouped_context = context.reshape(N_DP, TOKENS // N_DP, HQ)

    def add_group(running, pair):
        product = jnp.dot(pair[0].T, pair[1], preferred_element_type=jnp.float32).astype(jnp.bfloat16)
        return (running + product.astype(jnp.float32), None)
    weight_sum, unused_two = lax.scan(add_group, jnp.zeros((D, HQ), jnp.float32), (grouped_grads, grouped_context))
    weight_grad = weight_sum.astype(jnp.bfloat16)
    return (residual_grad, gate_grad, router_grad, gain_grad, context_grad, weight_grad)
```

```python
import functools

import jax
import jax.numpy as jnp
import numpy as np
from jax import lax
from jax.experimental import pallas as pl
from jax.experimental.pallas import tpu as pltpu
from jax.sharding import Mesh, PartitionSpec as P

CHIP = ("y", "x", "z")
EVERY = ("y", "x", "z", "core")
DP = ("y", "x")
TENSOR = ("z", "core")
SWAP = [(0, 1), (1, 0)]
WIDE = 512
SOME = 8
MIB = 1024 * 1024
bf16 = jnp.bfloat16
f32 = jnp.float32
OVER_ROWS = (((0,), (0,)), ((), ()))
OVER_LAST = (((1,), (1,)), ((), ()))


def swap_cores(value):
    return lax.ppermute(value, "core", SWAP)


def exchange(value, axes):
    return lax.all_to_all(value, axes, split_axis=0, concat_axis=0, tiled=True)


def pair_sum(value, axis):
    size = lax.axis_size(axis)
    for mask in (1, 3)[: size // 2]:
        value = value + lax.ppermute(value, axis, [(i, i ^ mask) for i in range(size)])
    return value


def ring_scatter(first, blocks, axis):
    size = lax.axis_size(axis)
    right = [(i, (i + 1) % size) for i in range(size)]
    left = [(i, (i - 1) % size) for i in range(size)]
    half = first.shape[0] // 2
    from_left = lax.ppermute(first[:half], axis, right)
    from_right = lax.ppermute(first[half:], axis, left)
    mine, after, before = blocks

    def joined(upper, lower, block):
        block = block.astype(f32)
        return jnp.concatenate([block[:half] + upper, block[half:] + lower], axis=0).astype(bf16)

    to_right = joined(from_left.astype(f32), 0.0, after)
    to_left = joined(0.0, from_right.astype(f32), before)
    got_left = lax.ppermute(to_right, axis, right)
    got_right = lax.ppermute(to_left, axis, left)
    return (mine.astype(f32) + got_left.astype(f32) + got_right.astype(f32)).astype(bf16)


def params(grid=0, mib=16):
    return pltpu.CompilerParams(
        vmem_limit_bytes=mib * MIB,
        dimension_semantics=("arbitrary",) * grid if grid else None,
    )


def slot_codes(routes_wide, experts, pieces, tok_rows):
    columns = pieces * tok_rows
    expert = lax.broadcasted_iota(jnp.int32, (experts, columns), 0)
    named = expert == routes_wide[0:1, :]
    for choice in range(1, routes_wide.shape[0]):
        named = named | (expert == routes_wide[choice : choice + 1, :])
    before = lax.broadcasted_iota(jnp.int32, (columns, columns), 0)
    after = lax.broadcasted_iota(jnp.int32, (columns, columns), 1)
    earlier = (before // tok_rows == after // tok_rows) & (before < after)
    rank = jnp.dot(
        jnp.where(named, 1.0, 0.0).astype(bf16),
        jnp.where(earlier, 1.0, 0.0).astype(bf16),
        preferred_element_type=f32,
    )
    piece = (lax.broadcasted_iota(jnp.int32, (experts, columns), 1) // tok_rows).astype(f32)
    return jnp.where(named, piece * 8.0 + rank, -1.0)


def row_codes(shape, capacity, block, dim):
    row = lax.broadcasted_iota(jnp.int32, shape, dim) % block
    return ((row // capacity) * 8 + row % capacity).astype(f32)


def place_kernel(
    capacity, pre_ref, grad_ref, gain_ref, routes_ref, send_ref, code_ref, normed_ref, source
):
    tok_rows, features = pre_ref.shape
    experts, columns = code_ref.shape
    pieces = features // WIDE
    block = pieces * capacity
    hidden = pre_ref[...].astype(f32)
    inverse = lax.rsqrt(jnp.mean(hidden * hidden, axis=-1, keepdims=True) + 1e-06)
    normed = (hidden * inverse * gain_ref[...]).astype(bf16)
    normed_ref[...] = normed
    for piece in range(pieces):
        at = pl.ds(piece * tok_rows, tok_rows)
        source[at, :WIDE] = normed[:, piece * WIDE : (piece + 1) * WIDE]
        source[at, WIDE:] = grad_ref[:, piece * WIDE : (piece + 1) * WIDE]
    code_ref[...] = slot_codes(routes_ref[...], experts, pieces, tok_rows)
    some = 8
    rows = some * block

    def step(group, carry):
        first = pl.multiple_of(group * some, some)
        code = code_ref[pl.ds(first, some), :]
        want = row_codes((some, block, columns), capacity, block, 1)
        hit = jnp.where(code[:, None, :] == want, 1.0, 0.0).astype(bf16).reshape(rows, columns)
        moved = jnp.dot(hit, source[...], preferred_element_type=f32).astype(bf16)
        send_ref[pl.ds(first, some), :block, :] = moved[:, :WIDE].reshape(some, block, WIDE)
        send_ref[pl.ds(first, some), block:, :] = moved[:, WIDE:].reshape(some, block, WIDE)
        return carry

    lax.fori_loop(0, experts // some, step, 0)


def place(pre_norm, out_grad, norm_gain, routes_wide, experts, capacity):
    tok_rows, features = pre_norm.shape
    pieces = features // WIDE
    block = pieces * capacity
    return pl.pallas_call(
        functools.partial(place_kernel, capacity),
        out_shape=(
            jax.ShapeDtypeStruct((experts, 2 * block, WIDE), bf16),
            jax.ShapeDtypeStruct((experts, pieces * tok_rows), f32),
            jax.ShapeDtypeStruct((tok_rows, features), bf16),
        ),
        scratch_shapes=[pltpu.VMEM((pieces * tok_rows, 2 * WIDE), bf16)],
        compiler_params=params(0, 24),
        name="place",
    )(pre_norm, out_grad, norm_gain, routes_wide)


def order_matrix(capacity, block):
    span = SOME * block
    to = lax.broadcasted_iota(jnp.int32, (span, span), 0)
    at = lax.broadcasted_iota(jnp.int32, (span, span), 1)
    moved = (at % block) // capacity * (SOME * capacity) + at // block * capacity + at % capacity
    return jnp.where(moved == to, 1.0, 0.0).astype(bf16)


def spread_kernel(capacity, got_ref, order_ref, rows_ref):
    some, block, _ = got_ref.shape
    pieces = block // capacity
    span = some * capacity
    source = got_ref[...].reshape(some * block, WIDE)
    moved = jnp.dot(order_ref[...], source, preferred_element_type=f32).astype(bf16)
    for piece in range(pieces):
        rows_ref[:, piece * WIDE : (piece + 1) * WIDE] = moved[piece * span : (piece + 1) * span]


def spread(got, kind, order, capacity):
    sources, double, _ = got.shape
    block = double // 2
    features = block // capacity * WIDE
    span = SOME * capacity
    return pl.pallas_call(
        functools.partial(spread_kernel, capacity),
        grid=(sources // SOME,),
        in_specs=[
            pl.BlockSpec((SOME, block, WIDE), lambda i: (i, kind, 0)),
            pl.BlockSpec(order.shape, lambda i: (0, 0)),
        ],
        out_specs=pl.BlockSpec((span, features), lambda i: (i, 0)),
        out_shape=jax.ShapeDtypeStruct((sources * capacity, features), bf16),
        compiler_params=params(1),
        name="spread",
    )(got, order)


def forward_kernel(own_ref, other_ref, gate_ref, up_ref, gate_pre_ref, up_pre_ref):
    count = own_ref.shape[0]
    units = gate_ref.shape[2]
    tile = 256
    for mat, out in ((gate_ref, gate_pre_ref), (up_ref, up_pre_ref)):
        for n in range(units // tile):
            at = slice(n * tile, (n + 1) * tile)
            out[:count, at] = jnp.dot(own_ref[...], mat[0, :, at], preferred_element_type=f32)
            out[count:, at] = jnp.dot(other_ref[...], mat[0, :, at], preferred_element_type=f32)


def forward(own, other, w_gate, w_up):
    count, features = own.shape
    units = w_gate.shape[2]
    inside = pl.BlockSpec(memory_space=pltpu.VMEM)
    return pl.pallas_call(
        forward_kernel,
        in_specs=[inside] * 4,
        out_specs=(inside, inside),
        out_shape=(jax.ShapeDtypeStruct((2 * count, units), f32),) * 2,
        compiler_params=params(),
        cost_estimate=pl.CostEstimate(
            flops=8 * count * features * units, bytes_accessed=24_000_000, transcendentals=0
        ),
        name="forward",
    )(own, other, w_gate, w_up)


def hidden_kernel(
    own_ref, other_ref, down_ref, gate_pre_ref, up_pre_ref, gg_ref, gu_ref, part_ref
):
    count = own_ref.shape[0]
    units = down_ref.shape[1]
    tile = 256
    for half, rows in enumerate((own_ref, other_ref)):
        here = slice(half * count, (half + 1) * count)
        part = jnp.zeros((count, 1), f32)
        for n in range(units // tile):
            at = slice(n * tile, (n + 1) * tile)
            upstream = lax.dot_general(
                rows[...], down_ref[0, at, :], OVER_LAST, preferred_element_type=f32
            )
            gate_pre = gate_pre_ref[here, at]
            up_pre = up_pre_ref[here, at]
            sig = jax.nn.sigmoid(gate_pre)
            grad_up = upstream * (gate_pre * sig)
            part = part + jnp.sum(grad_up * up_pre, axis=-1, keepdims=True)
            gu_ref[here, at] = grad_up.astype(bf16)
            gg_ref[here, at] = (
                upstream * up_pre * sig * (1.0 + gate_pre * (1.0 - sig))
            ).astype(bf16)
        part_ref[here, :] = jnp.broadcast_to(part.astype(bf16).astype(f32), (count, 128))


def hidden_grads(own, other, w_down, gate_pre, up_pre):
    count, features = own.shape
    units = w_down.shape[1]
    inside = pl.BlockSpec(memory_space=pltpu.VMEM)
    return pl.pallas_call(
        hidden_kernel,
        in_specs=[inside] * 5,
        out_specs=(inside, inside, inside),
        out_shape=(
            jax.ShapeDtypeStruct((2 * count, units), bf16),
            jax.ShapeDtypeStruct((2 * count, units), bf16),
            jax.ShapeDtypeStruct((2 * count, 128), f32),
        ),
        compiler_params=params(),
        cost_estimate=pl.CostEstimate(
            flops=4 * count * features * units, bytes_accessed=24_000_000, transcendentals=0
        ),
        name="hidden_grads",
    )(own, other, w_down, gate_pre, up_pre)


def term_kernel(gg_ref, gu_ref, gate_ref, up_ref, term_ref):
    features = gate_ref.shape[1]
    tile = 512
    for n in range(features // tile):
        at = slice(n * tile, (n + 1) * tile)
        term = lax.dot_general(
            gg_ref[...], gate_ref[0, at, :], OVER_LAST, preferred_element_type=f32
        )
        term = term + lax.dot_general(
            gu_ref[...], up_ref[0, at, :], OVER_LAST, preferred_element_type=f32
        )
        term_ref[:, at] = term.astype(bf16)


def terms(grad_gate, grad_up, w_gate, w_up, half):
    count = grad_gate.shape[0] // 2
    units = grad_gate.shape[1]
    features = w_gate.shape[1]
    inside = pl.BlockSpec(memory_space=pltpu.VMEM)
    return pl.pallas_call(
        term_kernel,
        in_specs=[inside] * 4,
        out_specs=inside,
        out_shape=jax.ShapeDtypeStruct((count, features), bf16),
        compiler_params=params(),
        cost_estimate=pl.CostEstimate(
            flops=4 * count * features * units, bytes_accessed=17_000_000, transcendentals=0
        ),
        name="terms",
    )(
        grad_gate[half * count : (half + 1) * count],
        grad_up[half * count : (half + 1) * count],
        w_gate,
        w_up,
    )


def pack_kernel(capacity, own_ref, other_ref, order_ref, send_ref, held):
    span, features = own_ref.shape
    pieces = features // WIDE
    for piece in range(pieces):
        at = slice(piece * WIDE, (piece + 1) * WIDE)
        held[pl.ds(piece * span, span), :] = (
            own_ref[:, at].astype(f32) + other_ref[:, at].astype(f32)
        ).astype(bf16)
    moved = lax.dot_general(order_ref[...], held[...], OVER_ROWS, preferred_element_type=f32)
    send_ref[...] = moved.astype(bf16).reshape(send_ref.shape)


def pack(own, other, order, capacity):
    count, features = own.shape
    block = features // WIDE * capacity
    span = SOME * capacity
    return pl.pallas_call(
        functools.partial(pack_kernel, capacity),
        grid=(count // span,),
        in_specs=[
            pl.BlockSpec((span, features), lambda i: (i, 0)),
            pl.BlockSpec((span, features), lambda i: (i, 0)),
            pl.BlockSpec(order.shape, lambda i: (0, 0)),
        ],
        out_specs=pl.BlockSpec((SOME, block, WIDE), lambda i: (i, 0, 0)),
        out_shape=jax.ShapeDtypeStruct((count // capacity, block, WIDE), bf16),
        scratch_shapes=[pltpu.VMEM((SOME * block, WIDE), bf16)],
        compiler_params=params(1),
        name="pack",
    )(own, other, order)


def mix_kernel(capacity, code_ref, gate_ref, mix_ref):
    some, columns = code_ref.shape
    rows = mix_ref.shape[1]
    block = rows // some
    want = row_codes((some, block, columns), capacity, block, 1)
    mixing = jnp.where(code_ref[...][:, None, :] == want, gate_ref[...][:, None, :], 0.0)
    mixing = mixing.reshape(rows, columns)
    high = mixing.astype(bf16)
    low = (mixing - high.astype(f32)).astype(bf16)
    mix_ref[:columns, :] = high.T
    mix_ref[columns:, :] = low.T


def mixings(code, gate_wide, capacity, block):
    experts, columns = code.shape
    some = 8
    return pl.pallas_call(
        functools.partial(mix_kernel, capacity),
        grid=(experts // some,),
        in_specs=[
            pl.BlockSpec((some, columns), lambda i: (i, 0)),
            pl.BlockSpec((some, columns), lambda i: (i, 0)),
        ],
        out_specs=pl.BlockSpec((2 * columns, some * block), lambda i: (0, i)),
        out_shape=jax.ShapeDtypeStruct((2 * columns, experts * block), bf16),
        compiler_params=params(1),
        name="mixings",
    )(code, gate_wide)


def finish_kernel(
    mix_ref, back_ref, pre_ref, grad_ref, gain_ref, logit_ref, router_ref,
    residual_ref, pieces_ref, gain_out_ref,
):
    tok_rows, features = pre_ref.shape
    columns = mix_ref.shape[0] // 2
    pieces = features // WIDE
    both = jnp.dot(mix_ref[...], back_ref[...], preferred_element_type=f32)
    expert_grad = both[:columns] + both[columns:]
    hidden = pre_ref[...].astype(f32)
    inverse = lax.rsqrt(jnp.mean(hidden * hidden, axis=-1, keepdims=True) + 1e-06)
    router_term = jnp.dot(logit_ref[...], router_ref[...], preferred_element_type=f32)
    moment = jnp.zeros((tok_rows, 1), f32)
    normed_grads = []
    for piece in range(pieces):
        at = slice(piece * WIDE, (piece + 1) * WIDE)
        normed_grad = (
            expert_grad[piece * tok_rows : (piece + 1) * tok_rows] + router_term[:, at]
        )
        normed_grads.append(normed_grad)
        gain_out_ref[:, at] = jnp.sum(
            normed_grad * hidden[:, at] * inverse, axis=0, keepdims=True
        )
        moment = moment + jnp.sum(
            hidden[:, at] * gain_ref[:, at] * normed_grad, axis=-1, keepdims=True
        )
    factor = inverse * inverse * inverse * (moment / features)
    for piece in range(pieces):
        at = slice(piece * WIDE, (piece + 1) * WIDE)
        residual = (
            grad_ref[:, at].astype(f32)
            + inverse * gain_ref[:, at] * normed_grads[piece]
            - hidden[:, at] * factor
        ).astype(bf16)
        residual_ref[:, at] = residual
        pieces_ref[pl.ds(piece * tok_rows, tok_rows), :] = residual


def finish(mix, back, pre_norm, out_grad, norm_gain, logit_full, router_wide):
    tok_rows, features = pre_norm.shape
    return pl.pallas_call(
        finish_kernel,
        out_shape=(
            jax.ShapeDtypeStruct((tok_rows, features), bf16),
            jax.ShapeDtypeStruct((tok_rows * features // WIDE, WIDE), bf16),
            jax.ShapeDtypeStruct((1, features), f32),
        ),
        compiler_params=params(0, 24),
        name="finish",
    )(mix, back, pre_norm, out_grad, norm_gain, logit_full, router_wide)


def shards(
    pre_norm,
    out_grad,
    routes,
    gate_probs,
    norm_gain,
    router_weight,
    w_gate,
    w_up,
    w_down,
    context,
    out_weight,
):
    tok_rows, features = pre_norm.shape
    top = routes.shape[1]
    experts = router_weight.shape[1]
    capacity = tok_rows * top * 3 // (2 * experts)
    pieces = features // WIDE
    block = pieces * capacity
    gain = norm_gain.reshape(1, features)

    routes_wide = jnp.tile(routes.T, (1, pieces))
    send, code, normed = place(pre_norm, out_grad, gain, routes_wide, experts, capacity)

    got = exchange(send, CHIP)

    order = order_matrix(capacity, block)
    named = routes[:, :, None] == jnp.arange(experts, dtype=jnp.int32)[None, None, :]
    gate_of = jnp.sum(jnp.where(named, gate_probs[:, :, None], 0.0), axis=1)
    mix = mixings(code, jnp.tile(gate_of.T, (1, pieces)), capacity, block)
    router_wide = router_weight.T
    got, order, mix, router_wide, out_weight, context = lax.optimization_barrier(
        (got, order, mix, router_wide, out_weight, context)
    )

    weight_band = lax.all_gather(out_weight, "x", axis=0, tiled=True)
    context_band = lax.all_gather(context, "y", axis=0, tiled=True)

    own_tokens = spread(got, 0, order, capacity)
    other_tokens = swap_cores(own_tokens)
    own_grads = spread(got, 1, order, capacity)
    other_grads = swap_cores(own_grads)
    gate_pre, up_pre = forward(own_tokens, other_tokens, w_gate, w_up)
    grad_gate, grad_up, part = hidden_grads(own_grads, other_grads, w_down, gate_pre, up_pre)
    count = part.shape[0] // 2
    part = part[:count] + swap_cores(part[count:])
    part = jnp.pad(part.reshape(experts, capacity, 128), ((0, 0), (0, 8 - capacity), (0, 0)))
    part = exchange(part, CHIP)[:, :capacity, 0]

    other_term = terms(grad_gate, grad_up, w_gate, w_up, 1)
    grad_gate, other_term = lax.optimization_barrier((grad_gate, other_term))
    own_term = terms(grad_gate, grad_up, w_gate, w_up, 0)
    send_back = pack(own_term, swap_cores(other_term), order, capacity)
    send_back, weight_band, context_band = lax.optimization_barrier(
        (send_back, weight_band, context_band)
    )
    got_back = exchange(send_back, CHIP).reshape(experts * block, WIDE)

    slot = code[:, :tok_rows].T
    at_slot = jnp.arange(capacity, dtype=jnp.int32).astype(f32)
    grad_of = jnp.sum(
        jnp.where(slot[:, :, None] == at_slot[None, None, :], part[None], 0.0), axis=2
    )
    gate_grad = jnp.sum(jnp.where(named, grad_of[:, None, :], 0.0), axis=2)
    weighted = jnp.sum(gate_of * grad_of, axis=-1, keepdims=True)
    logit_full = (gate_of * (grad_of - weighted)).astype(bf16)
    router_part = lax.dot_general(normed, logit_full, OVER_ROWS, preferred_element_type=f32)
    router_sum = lax.psum_scatter(router_part, TENSOR, scatter_dimension=0, tiled=True)
    got_back, router_sum = lax.optimization_barrier((got_back, router_sum))

    residual_grad, residual, gain_part = finish(
        mix, got_back, pre_norm, out_grad, gain, logit_full, router_wide
    )

    sides = lax.axis_size("y")
    shared = lax.axis_size(TENSOR)
    band = features // shared
    swapped = exchange(residual.reshape(sides, -1, WIDE), "y")
    gathered = lax.all_gather(swapped, TENSOR, axis=0, tiled=False)

    gain_all = gain_part.reshape(features // 128, 128)
    gain_all = pair_sum(pair_sum(gain_all, "core"), "z")
    per = band // 128
    mine = lax.dynamic_slice_in_dim(gain_all, lax.axis_index(TENSOR) * per, per, 0)
    small = jnp.concatenate([router_sum.reshape(-1, 128), mine], axis=0)
    small = pair_sum(pair_sum(small, "x"), "y")
    router_grad = small[:-per].reshape(band, experts)
    gain_grad = small[-per:].reshape(band)
    gathered, small = lax.optimization_barrier((gathered, small))

    square = gathered.reshape(shared, sides, pieces // sides, tok_rows, WIDE)
    square = square.transpose(1, 0, 3, 2, 4).reshape(sides, shared * tok_rows, features // sides)
    row, column = lax.axis_index("y"), lax.axis_index("x")

    def context_block(step):
        rows = lax.dynamic_index_in_dim(square, lax.rem(row + step, sides), 0, keepdims=False)
        return jnp.dot(rows, weight_band, preferred_element_type=f32).astype(bf16)

    opposite = context_block(2)
    context_grad = ring_scatter(
        opposite, (context_block(0), context_block(1), context_block(3)), "y"
    )
    weight_part = lax.dot_general(
        square.reshape(sides * shared * tok_rows, features // sides),
        context_band,
        OVER_ROWS,
        preferred_element_type=f32,
    ).astype(bf16)
    weight_part = weight_part.reshape(sides, -1, weight_part.shape[1])

    def weight_block(step):
        return lax.dynamic_index_in_dim(
            weight_part, lax.rem(column + step, sides), 0, keepdims=False
        )

    weight_grad = ring_scatter(
        weight_block(2), (weight_block(0), weight_block(1), weight_block(3)), "x"
    )
    return (residual_grad, gate_grad, router_grad, gain_grad, context_grad, weight_grad)


def solution(mesh):
    devices = np.asarray(mesh.devices)
    fine = Mesh(devices.reshape(4, 4, 4, 2), EVERY)
    rows = P(EVERY, None)
    cube = P(EVERY, None, None)
    split = P(DP, TENSOR)
    return jax.shard_map(
        shards,
        mesh=fine,
        in_specs=(rows, rows, rows, rows, P(), P(), cube, cube, cube, split, split),
        out_specs=(rows, rows, P(TENSOR, None), P(TENSOR), split, split),
        check_vma=False,
    )
```

```python
import functools

import jax
import jax.numpy as jnp
import numpy as np
from jax import lax
from jax.experimental import pallas as pl
from jax.experimental.pallas import tpu as pltpu
from jax.sharding import Mesh, PartitionSpec as P

CHIP = ("y", "x", "z")
EVERY = ("y", "x", "z", "core")
DP = ("y", "x")
TENSOR = ("z", "core")
SWAP = [(0, 1), (1, 0)]
WIDE = 512
SOME = 8
MIB = 1024 * 1024
bf16 = jnp.bfloat16
f32 = jnp.float32
OVER_ROWS = (((0,), (0,)), ((), ()))
OVER_LAST = (((1,), (1,)), ((), ()))


def swap_cores(value):
    return lax.ppermute(value, "core", SWAP)


def exchange(value, axes):
    return lax.all_to_all(value, axes, split_axis=0, concat_axis=0, tiled=True)


def cross_sum(value, axis):
    size = lax.axis_size(axis)
    value = value.astype(bf16)
    one, two, three = [
        lax.ppermute(value, axis, [(i, i ^ mask) for i in range(size)]) for mask in (1, 2, 3)
    ]
    return (value.astype(f32) + two.astype(f32)) + (one.astype(f32) + three.astype(f32))


def shift(value, axis, step):
    size = lax.axis_size(axis)
    return lax.ppermute(value, axis, [(i, (i + step) % size) for i in range(size)])


def pass_on_kernel(*refs):
    ins, outs = refs[: len(refs) * 2 // 3], refs[len(refs) * 2 // 3 :]
    for at, out in enumerate(outs):
        here, came = ins[2 * at], ins[2 * at + 1]
        half = here.shape[0]
        first = (at % 2) * half
        came = came[first : first + half, :]
        out[...] = (here[...].astype(f32) + came.astype(f32)).astype(bf16)


def close_kernel(*refs):
    ins, outs = refs[:-2], refs[-2:]
    for at, out in enumerate(outs):
        upper, lower, from_left, from_right, last_left, last_right = ins[6 * at : 6 * at + 6]
        half = upper.shape[0]
        out[:half, :] = (
            upper[...].astype(f32) + from_right[:half, :].astype(f32) + last_left[...].astype(f32)
        ).astype(bf16)
        out[half:, :] = (
            lower[...].astype(f32) + from_left[half:, :].astype(f32) + last_right[...].astype(f32)
        ).astype(bf16)


def whole_call(kernel, name, shapes, *arrays):
    whole = pl.BlockSpec(memory_space=pltpu.VMEM)
    return pl.pallas_call(
        kernel,
        in_specs=[whole] * len(arrays),
        out_specs=tuple(whole for _ in shapes),
        out_shape=tuple(jax.ShapeDtypeStruct(shape, bf16) for shape in shapes),
        compiler_params=params(0, 16),
        name=name,
    )(*arrays)


def ring_scatter(square, rings, small):
    places = [lax.axis_index(axis).astype(jnp.int32).reshape(1) for _, _, axis in rings]
    firsts = [
        kernel(place, square, band, (((2, 0), (1, 1)), ((3, 0), (2, 1))))
        for place, (kernel, band, _) in zip(places, rings)
    ]
    firsts, small = lax.optimization_barrier((firsts, small))
    sent = [
        (shift(to_right, axis, 1), shift(to_left, axis, -1))
        for (to_right, to_left), (_, _, axis) in zip(firsts, rings)
    ]
    rests = [
        kernel(place, square, band, (((1, 0),), ((3, 1),), ((0, 0),), ((0, 1),)))
        for place, (kernel, band, _) in zip(places, rings)
    ]
    sent, rests = lax.optimization_barrier((sent, rests))
    half, width = rests[0][0].shape
    passed = whole_call(
        pass_on_kernel,
        "pass_on",
        [(half, width)] * 4,
        *[
            v
            for came, rest in zip(sent, rests)
            for v in (rest[0], *outside(came[0]), rest[1], *outside(came[1]))
        ],
    )
    last = []
    for at, (_, _, axis) in enumerate(rings):
        last.append((shift(passed[2 * at], axis, 1), shift(passed[2 * at + 1], axis, -1)))
    sums = whole_call(
        close_kernel,
        "close",
        [(2 * half, width)] * 2,
        *[
            v
            for came, rest, end in zip(sent, rests, last)
            for v in (rest[2], rest[3], *outside(*came, *end))
        ],
    )
    return (*sums, small)


def gather_kernel(place_ref, *refs):
    *pieces, out_ref, sems = refs
    sides, tok_rows, _ = pieces[0].shape
    y, z, core = place_ref[0], place_ref[1], place_ref[2]
    copies = []
    for at, piece in enumerate(pieces):
        side, turn = at // sides, at % sides
        here = lax.rem(z - turn + sides, sides) * 2 + (core if side == 0 else 1 - core)
        rows = pl.ds(pl.multiple_of(here * tok_rows, tok_rows), tok_rows)
        for back in range(sides):
            copies.append(
                pltpu.make_async_copy(
                    piece.at[back],
                    out_ref.at[lax.rem(y - back + sides, sides), rows],
                    sems.at[at * sides + back],
                )
            )
    for copy in copies:
        copy.start()
    for copy in copies:
        copy.wait()


def gather_square(bands, small):
    sides, tok_rows, width = bands.shape
    y, z, core = lax.axis_index("y"), lax.axis_index("z"), lax.axis_index("core")

    def block(value, index):
        return lax.dynamic_index_in_dim(value, index, 0, keepdims=False)

    own = block(bands, y)
    piece = [own] + [
        shift(block(bands, lax.rem(y + step, sides)), "y", step) for step in range(1, sides)
    ]
    small = small.reshape(sides, 2, *small.shape[1:])
    mine = lax.dynamic_index_in_dim(small, core, 1, keepdims=False)
    theirs = lax.dynamic_index_in_dim(small, 1 - core, 1, keepdims=False)
    small = mine + swap_cores(theirs.astype(bf16)).astype(f32)
    piece = jnp.stack(piece)
    piece, small = lax.optimization_barrier((piece, small))
    passed = small.astype(bf16)
    came = [
        shift(block(passed, lax.rem(z + step, sides)), "z", step) for step in range(1, sides)
    ]
    near = [piece] + [shift(piece, "z", step) for step in (1, 3, 2)]
    far = [swap_cores(p) for p in near]
    small = block(small, z) + sum(c.astype(f32) for c in came)
    small = cross_sum(small, "x")
    near, far, small = lax.optimization_barrier((near, far, small))
    small = cross_sum(small, "y")
    near = [near[0], near[1], near[3], near[2]]
    far = [far[0], far[1], far[3], far[2]]
    whole = pl.BlockSpec(memory_space=pltpu.VMEM)
    square = pl.pallas_call(
        gather_kernel,
        in_specs=[pl.BlockSpec(memory_space=pltpu.SMEM)]
        + [pl.BlockSpec(memory_space=pl.ANY)] * (2 * sides),
        out_specs=whole,
        out_shape=jax.ShapeDtypeStruct((sides, 2 * sides * tok_rows, width), bf16),
        scratch_shapes=[pltpu.SemaphoreType.DMA((2 * sides * sides,))],
        compiler_params=params(0, 16),
        name="gather_square",
    )(jnp.stack([y, z, core]).astype(jnp.int32), *near, *far)
    return square, small


def context_kernel(wanted, place_ref, square_ref, band_ref, *out_refs):
    sides, tokens, _ = square_ref.shape
    half = tokens // 2
    for blocks, out_ref in zip(wanted, out_refs):
        for at, (step, part) in enumerate(blocks):
            block = lax.rem(place_ref[0] + step, sides)
            rows = square_ref[pl.ds(block, 1), part * half : (part + 1) * half, :][0]
            out_ref[at * half : (at + 1) * half, :] = jnp.dot(
                rows, band_ref[...], preferred_element_type=f32
            ).astype(bf16)


def weight_kernel(wanted, place_ref, square_ref, band_ref, *out_refs):
    sides, tokens, depth = square_ref.shape
    half = depth // sides // 2
    for blocks, out_ref in zip(wanted, out_refs):
        for at, (step, part) in enumerate(blocks):
            block = lax.rem(place_ref[0] + step, sides)
            columns = pl.ds(pl.multiple_of((2 * block + part) * half, half), half)
            out_ref[at * half : (at + 1) * half, :] = lax.dot_general(
                square_ref[:, :, columns].reshape(sides * tokens, half),
                band_ref[...],
                OVER_ROWS,
                preferred_element_type=f32,
            ).astype(bf16)


def projection(kernel, name, place, square, band, wanted):
    width = band.shape[1]
    half = square.shape[1] // 2
    count = sum(len(blocks) for blocks in wanted)
    whole = pl.BlockSpec(memory_space=pltpu.VMEM)
    return pl.pallas_call(
        functools.partial(kernel, wanted),
        in_specs=[pl.BlockSpec(memory_space=pltpu.SMEM), whole, whole],
        out_specs=tuple(whole for _ in wanted),
        out_shape=tuple(
            jax.ShapeDtypeStruct((half * len(blocks), width), bf16) for blocks in wanted
        ),
        compiler_params=params(0, 16),
        cost_estimate=pl.CostEstimate(
            flops=2 * half * count * band.shape[0] * width,
            bytes_accessed=5_000_000,
            transcendentals=0,
        ),
        name=name,
    )(place, square, *kept(band))


def kept(*arrays):
    return [pltpu.with_memory_space_constraint(a, pltpu.VMEM) for a in arrays]


def outside(*arrays):
    return [pltpu.with_memory_space_constraint(a, pltpu.HBM) for a in arrays]


def params(grid=0, mib=16):
    return pltpu.CompilerParams(
        vmem_limit_bytes=mib * MIB,
        dimension_semantics=("arbitrary",) * grid if grid else None,
    )


def slot_codes(routes_wide, experts, pieces, tok_rows):
    columns = pieces * tok_rows
    expert = lax.broadcasted_iota(jnp.int32, (experts, columns), 0)
    named = expert == routes_wide[0:1, :]
    for choice in range(1, routes_wide.shape[0]):
        named = named | (expert == routes_wide[choice : choice + 1, :])
    before = lax.broadcasted_iota(jnp.int32, (columns, columns), 0)
    after = lax.broadcasted_iota(jnp.int32, (columns, columns), 1)
    earlier = (before // tok_rows == after // tok_rows) & (before < after)
    rank = jnp.dot(
        jnp.where(named, 1.0, 0.0).astype(bf16),
        jnp.where(earlier, 1.0, 0.0).astype(bf16),
        preferred_element_type=f32,
    )
    piece = (lax.broadcasted_iota(jnp.int32, (experts, columns), 1) // tok_rows).astype(f32)
    return jnp.where(named, piece * 8.0 + rank, -1.0)


def row_codes(shape, capacity, block, dim):
    row = lax.broadcasted_iota(jnp.int32, shape, dim) % block
    return ((row // capacity) * 8 + row % capacity).astype(f32)


def place_kernel(
    capacity, pre_ref, grad_ref, gain_ref, routes_ref, send_ref, code_ref, normed_ref, source
):
    tok_rows, features = pre_ref.shape
    experts, columns = code_ref.shape
    pieces = features // WIDE
    block = pieces * capacity
    group = pl.program_id(0)
    some = send_ref.shape[0]
    rows = some * block

    @pl.when(group == 0)
    def prepare():
        hidden = pre_ref[...].astype(f32)
        inverse = lax.rsqrt(jnp.mean(hidden * hidden, axis=-1, keepdims=True) + 1e-06)
        normed = (hidden * inverse * gain_ref[...]).astype(bf16)
        normed_ref[...] = normed
        for piece in range(pieces):
            at = pl.ds(piece * tok_rows, tok_rows)
            source[at, :WIDE] = normed[:, piece * WIDE : (piece + 1) * WIDE]
            source[at, WIDE:] = grad_ref[:, piece * WIDE : (piece + 1) * WIDE]
        code_ref[...] = slot_codes(routes_ref[...], experts, pieces, tok_rows)

    code = code_ref[pl.ds(pl.multiple_of(group * some, some), some), :]
    want = row_codes((some, block, columns), capacity, block, 1)
    hit = jnp.where(code[:, None, :] == want, 1.0, 0.0).astype(bf16).reshape(rows, columns)
    moved = jnp.dot(hit, source[...], preferred_element_type=f32).astype(bf16)
    send_ref[:, :block, :] = moved[:, :WIDE].reshape(some, block, WIDE)
    send_ref[:, block:, :] = moved[:, WIDE:].reshape(some, block, WIDE)


def place(pre_norm, out_grad, norm_gain, routes_wide, experts, capacity):
    tok_rows, features = pre_norm.shape
    pieces = features // WIDE
    block = pieces * capacity
    some = 8
    columns = pieces * tok_rows

    def whole(*shape):
        return pl.BlockSpec(shape, lambda i: (0,) * len(shape))

    return pl.pallas_call(
        functools.partial(place_kernel, capacity),
        grid=(experts // some,),
        in_specs=[
            whole(tok_rows, features),
            whole(tok_rows, features),
            whole(1, features),
            whole(*routes_wide.shape),
        ],
        out_specs=(
            pl.BlockSpec((some, 2 * block, WIDE), lambda i: (i, 0, 0)),
            whole(experts, columns),
            whole(tok_rows, features),
        ),
        out_shape=(
            pltpu.HBM((experts, 2 * block, WIDE), bf16),
            jax.ShapeDtypeStruct((experts, columns), f32),
            jax.ShapeDtypeStruct((tok_rows, features), bf16),
        ),
        scratch_shapes=[pltpu.VMEM((columns, 2 * WIDE), bf16)],
        compiler_params=params(1, 16),
        name="place",
    )(*outside(pre_norm, out_grad, norm_gain), routes_wide)


def order_matrix(capacity, block):
    at = np.arange(SOME * block)
    moved = (at % block) // capacity * (SOME * capacity) + at // block * capacity + at % capacity
    return jnp.asarray(moved[None, :] == at[:, None], bf16)


def spread_kernel(capacity, got_ref, order_ref, rows_ref):
    some, block, _ = got_ref.shape
    pieces = block // capacity
    span = SOME * capacity
    for group in range(some // SOME):
        source = got_ref[group * SOME : (group + 1) * SOME].reshape(SOME * block, WIDE)
        moved = jnp.dot(order_ref[...], source, preferred_element_type=f32).astype(bf16)
        for piece in range(pieces):
            rows_ref[group * span : (group + 1) * span, piece * WIDE : (piece + 1) * WIDE] = moved[
                piece * span : (piece + 1) * span
            ]


def spread(got, kind, order, capacity):
    sources, double, _ = got.shape
    block = double // 2
    features = block // capacity * WIDE
    some = 2 * SOME
    return pl.pallas_call(
        functools.partial(spread_kernel, capacity),
        grid=(sources // some,),
        in_specs=[
            pl.BlockSpec((some, block, WIDE), lambda i: (i, kind, 0)),
            pl.BlockSpec(order.shape, lambda i: (0, 0)),
        ],
        out_specs=pl.BlockSpec((some * capacity, features), lambda i: (i, 0)),
        out_shape=jax.ShapeDtypeStruct((sources * capacity, features), bf16),
        compiler_params=params(1),
        name="spread",
    )(got, order)


def forward_kernel(own_ref, other_ref, gate_ref, up_ref, gate_pre_ref, up_pre_ref):
    count = own_ref.shape[0]
    units = gate_ref.shape[2]
    tile = 256
    for mat, out in ((gate_ref, gate_pre_ref), (up_ref, up_pre_ref)):
        for n in range(units // tile):
            at = slice(n * tile, (n + 1) * tile)
            out[:count, at] = jnp.dot(own_ref[...], mat[0, :, at], preferred_element_type=f32)
            out[count:, at] = jnp.dot(other_ref[...], mat[0, :, at], preferred_element_type=f32)


def forward(own, other, w_gate, w_up):
    count, features = own.shape
    units = w_gate.shape[2]
    inside = pl.BlockSpec(memory_space=pltpu.VMEM)
    return pl.pallas_call(
        forward_kernel,
        in_specs=[inside] * 4,
        out_specs=(inside, inside),
        out_shape=(jax.ShapeDtypeStruct((2 * count, units), f32),) * 2,
        compiler_params=params(0, 10),
        cost_estimate=pl.CostEstimate(
            flops=8 * count * features * units, bytes_accessed=24_000_000, transcendentals=0
        ),
        name="forward",
    )(own, other, *kept(w_gate, w_up))


def hidden_kernel(
    capacity, own_ref, other_ref, down_ref, gate_pre_ref, up_pre_ref, gg_ref, gu_ref, *part_refs
):
    count = own_ref.shape[0]
    units = down_ref.shape[1]
    tile = 256
    for half, rows in enumerate((own_ref, other_ref)):
        here = slice(half * count, (half + 1) * count)
        part = jnp.zeros((count, 1), f32)
        for n in range(units // tile):
            at = slice(n * tile, (n + 1) * tile)
            upstream = lax.dot_general(
                rows[...], down_ref[0, at, :], OVER_LAST, preferred_element_type=f32
            )
            gate_pre = gate_pre_ref[here, at]
            up_pre = up_pre_ref[here, at]
            sig = jax.nn.sigmoid(gate_pre)
            grad_up = upstream * (gate_pre * sig)
            part = part + jnp.sum(grad_up * up_pre, axis=-1, keepdims=True)
            gu_ref[here, at] = grad_up.astype(bf16)
            gg_ref[here, at] = (
                upstream * up_pre * sig * (1.0 + gate_pre * (1.0 - sig))
            ).astype(bf16)
        part_rows = part_refs[half].shape[0]
        rows_of = lax.broadcasted_iota(jnp.int32, (part_rows, count), 0)
        slots_of = lax.broadcasted_iota(jnp.int32, (part_rows, count), 1)
        same = (rows_of // 8 == slots_of // capacity) & (rows_of % 8 == slots_of % capacity)
        part_refs[half][...] = jnp.dot(
            jnp.where(same, 1.0, 0.0).astype(bf16),
            jnp.broadcast_to(part.astype(bf16), (count, 128)),
            preferred_element_type=f32,
        )


def hidden_grads(own, other, w_down, gate_pre, up_pre, capacity):
    count, features = own.shape
    units = w_down.shape[1]
    inside = pl.BlockSpec(memory_space=pltpu.VMEM)
    return pl.pallas_call(
        functools.partial(hidden_kernel, capacity),
        in_specs=[inside] * 5,
        out_specs=(inside,) * 4,
        out_shape=(
            jax.ShapeDtypeStruct((2 * count, units), bf16),
            jax.ShapeDtypeStruct((2 * count, units), bf16),
            jax.ShapeDtypeStruct((count // capacity * 8, 128), f32),
            jax.ShapeDtypeStruct((count // capacity * 8, 128), f32),
        ),
        compiler_params=params(0, 10),
        cost_estimate=pl.CostEstimate(
            flops=4 * count * features * units, bytes_accessed=24_000_000, transcendentals=0
        ),
        name="hidden_grads",
    )(own, other, *kept(w_down), gate_pre, up_pre)


def term_kernel(half, gg_ref, gu_ref, gate_ref, up_ref, term_ref):
    count = term_ref.shape[0]
    here = slice(half * count, (half + 1) * count)
    features = gate_ref.shape[1]
    tile = 512
    for n in range(features // tile):
        at = slice(n * tile, (n + 1) * tile)
        term = lax.dot_general(
            gg_ref[here, :], gate_ref[0, at, :], OVER_LAST, preferred_element_type=f32
        )
        term = term + lax.dot_general(
            gu_ref[here, :], up_ref[0, at, :], OVER_LAST, preferred_element_type=f32
        )
        term_ref[:, at] = term.astype(bf16)


def terms(grad_gate, grad_up, w_gate, w_up, half):
    count = grad_gate.shape[0] // 2
    units = grad_gate.shape[1]
    features = w_gate.shape[1]
    inside = pl.BlockSpec(memory_space=pltpu.VMEM)
    return pl.pallas_call(
        functools.partial(term_kernel, half),
        in_specs=[inside] * 4,
        out_specs=inside,
        out_shape=jax.ShapeDtypeStruct((count, features), bf16),
        compiler_params=params(0, 10),
        cost_estimate=pl.CostEstimate(
            flops=4 * count * features * units, bytes_accessed=17_000_000, transcendentals=0
        ),
        name="terms",
    )(grad_gate, grad_up, *kept(w_gate, w_up))


def pack_kernel(capacity, own_ref, other_ref, order_ref, send_ref, held):
    rows, features = own_ref.shape
    pieces = features // WIDE
    span = SOME * capacity
    for group in range(rows // span):
        here = slice(group * span, (group + 1) * span)
        for piece in range(pieces):
            at = slice(piece * WIDE, (piece + 1) * WIDE)
            held[group, pl.ds(piece * span, span), :] = (
                own_ref[here, at].astype(f32) + other_ref[here, at].astype(f32)
            ).astype(bf16)
        moved = lax.dot_general(
            order_ref[...], held[group], OVER_ROWS, preferred_element_type=f32
        )
        send_ref[group * SOME : (group + 1) * SOME] = moved.astype(bf16).reshape(
            SOME, -1, WIDE
        )


def pack(own, other, order, capacity):
    count, features = own.shape
    block = features // WIDE * capacity
    groups = 2
    span = groups * SOME * capacity
    return pl.pallas_call(
        functools.partial(pack_kernel, capacity),
        grid=(count // span,),
        in_specs=[
            pl.BlockSpec((span, features), lambda i: (i, 0)),
            pl.BlockSpec((span, features), lambda i: (i, 0)),
            pl.BlockSpec(order.shape, lambda i: (0, 0)),
        ],
        out_specs=pl.BlockSpec((groups * SOME, block, WIDE), lambda i: (i, 0, 0)),
        out_shape=pltpu.HBM((count // capacity, block, WIDE), bf16),
        scratch_shapes=[pltpu.VMEM((groups, SOME * block, WIDE), bf16)],
        compiler_params=params(1),
        name="pack",
    )(own, other, order)


def mix_kernel(capacity, code_ref, gate_ref, mix_ref):
    some, columns = code_ref.shape
    rows = mix_ref.shape[1]
    block = rows // some
    want = row_codes((some, block, columns), capacity, block, 1)
    mixing = jnp.where(code_ref[...][:, None, :] == want, gate_ref[...][:, None, :], 0.0)
    mixing = mixing.reshape(rows, columns)
    high = mixing.astype(bf16)
    low = (mixing - high.astype(f32)).astype(bf16)
    mix_ref[:columns, :] = high.T
    mix_ref[columns:, :] = low.T


def mixings(code, gate_wide, capacity, block):
    experts, columns = code.shape
    some = 8
    return pl.pallas_call(
        functools.partial(mix_kernel, capacity),
        grid=(experts // some,),
        in_specs=[
            pl.BlockSpec((some, columns), lambda i: (i, 0)),
            pl.BlockSpec((some, columns), lambda i: (i, 0)),
        ],
        out_specs=pl.BlockSpec((2 * columns, some * block), lambda i: (0, i)),
        out_shape=jax.ShapeDtypeStruct((2 * columns, experts * block), bf16),
        compiler_params=params(1),
        name="mixings",
    )(code, gate_wide)


def finish_kernel(
    mix_ref, back_ref, pre_ref, grad_ref, gain_ref, logit_ref, router_ref, normed_ref,
    residual_ref, bands_ref, small_ref,
):
    tok_rows, features = pre_ref.shape
    columns = mix_ref.shape[0] // 2
    pieces = features // WIDE
    both = jnp.dot(mix_ref[...], back_ref[...], preferred_element_type=f32)
    expert_grad = both[:columns] + both[columns:]
    hidden = pre_ref[...].astype(f32)
    inverse = lax.rsqrt(jnp.mean(hidden * hidden, axis=-1, keepdims=True) + 1e-06)
    router_term = jnp.dot(logit_ref[...], router_ref[...], preferred_element_type=f32)
    experts = logit_ref.shape[1]
    router_part = lax.dot_general(
        logit_ref[...], normed_ref[...], OVER_ROWS, preferred_element_type=f32
    )
    spare = small_ref.shape[1] - experts
    per_band = bands_ref.shape[2] // WIDE
    moment = jnp.zeros((tok_rows, 1), f32)
    normed_grads = []
    for piece in range(pieces):
        at = slice(piece * WIDE, (piece + 1) * WIDE)
        normed_grad = (
            expert_grad[piece * tok_rows : (piece + 1) * tok_rows] + router_term[:, at]
        )
        normed_grads.append(normed_grad)
        small_ref[piece, :experts, :] = router_part[:, at]
        small_ref[piece, experts:, :] = jnp.broadcast_to(
            jnp.sum(normed_grad * hidden[:, at] * inverse, axis=0, keepdims=True), (spare, WIDE)
        )
        moment = moment + jnp.sum(
            hidden[:, at] * gain_ref[:, at] * normed_grad, axis=-1, keepdims=True
        )
    factor = inverse * inverse * inverse * (moment / features)
    for piece in range(pieces):
        at = slice(piece * WIDE, (piece + 1) * WIDE)
        residual = (
            grad_ref[:, at].astype(f32)
            + inverse * gain_ref[:, at] * normed_grads[piece]
            - hidden[:, at] * factor
        ).astype(bf16)
        residual_ref[:, at] = residual
        inner = piece % per_band * WIDE
        bands_ref[piece // per_band, :, inner : inner + WIDE] = residual


def finish(mix, back, pre_norm, out_grad, norm_gain, logit_full, router_wide, normed, bands):
    tok_rows, features = pre_norm.shape
    experts = logit_full.shape[1]
    return pl.pallas_call(
        finish_kernel,
        out_shape=(
            jax.ShapeDtypeStruct((tok_rows, features), bf16),
            jax.ShapeDtypeStruct((bands, tok_rows, features // bands), bf16),
            jax.ShapeDtypeStruct((features // WIDE, experts + 8, WIDE), f32),
        ),
        compiler_params=params(0, 24),
        name="finish",
    )(
        mix,
        *outside(back, pre_norm, out_grad, norm_gain),
        logit_full,
        router_wide,
        *outside(normed),
    )


def shards(
    pre_norm,
    out_grad,
    routes,
    gate_probs,
    norm_gain,
    router_weight,
    w_gate,
    w_up,
    w_down,
    context,
    out_weight,
):
    tok_rows, features = pre_norm.shape
    top = routes.shape[1]
    experts = router_weight.shape[1]
    capacity = tok_rows * top * 3 // (2 * experts)
    pieces = features // WIDE
    block = pieces * capacity
    gain = norm_gain.reshape(1, features)

    routes_wide = jnp.tile(routes.T, (1, pieces))
    send, code, normed = place(pre_norm, out_grad, gain, routes_wide, experts, capacity)

    got = exchange(send, CHIP)

    order = order_matrix(capacity, block)
    got, code, normed, out_weight, context, routes, gate_probs = lax.optimization_barrier(
        (got, code, normed, out_weight, context, routes, gate_probs)
    )

    weight_band = lax.all_gather(out_weight, "x", axis=0, tiled=True)
    context_band = lax.all_gather(context, "y", axis=0, tiled=True)

    own_tokens = spread(got, 0, order, capacity)
    other_tokens = swap_cores(own_tokens)
    own_grads = spread(got, 1, order, capacity)
    other_grads = swap_cores(own_grads)
    gate_pre, up_pre = forward(own_tokens, other_tokens, w_gate, w_up)
    grad_gate, grad_up, own_part, other_part = hidden_grads(
        own_grads, other_grads, w_down, gate_pre, up_pre, capacity
    )
    grad_gate, weight_band = lax.optimization_barrier((grad_gate, weight_band))
    other_part = swap_cores(other_part)
    other_term = terms(grad_gate, grad_up, w_gate, w_up, 1)
    other_term = swap_cores(other_term)
    own_term = terms(grad_gate, grad_up, w_gate, w_up, 0)
    own_term, context_band = lax.optimization_barrier((own_term, context_band))
    send_back = pack(own_term, other_term, order, capacity)
    send_back, own_part, other_part = lax.optimization_barrier(
        (send_back, own_part, other_part)
    )
    part = (own_part + other_part).reshape(experts, 8, 128)
    part = exchange(part, CHIP)[:, :capacity, 0]
    send_back, part, code, routes, gate_probs, router_weight = lax.optimization_barrier(
        (send_back, part, code, routes, gate_probs, router_weight)
    )
    got_back = exchange(send_back, CHIP).reshape(experts * block, WIDE)

    named = routes[:, :, None] == jnp.arange(experts, dtype=jnp.int32)[None, None, :]
    gate_of = jnp.sum(jnp.where(named, gate_probs[:, :, None], 0.0), axis=1)
    mix = mixings(code, jnp.tile(gate_of.T, (1, pieces)), capacity, block)
    router_wide = router_weight.T

    slot = code[:, :tok_rows].T
    at_slot = jnp.arange(capacity, dtype=jnp.int32).astype(f32)
    grad_of = jnp.sum(
        jnp.where(slot[:, :, None] == at_slot[None, None, :], part[None], 0.0), axis=2
    )
    gate_grad = jnp.sum(jnp.where(named, grad_of[:, None, :], 0.0), axis=2)
    weighted = jnp.sum(gate_of * grad_of, axis=-1, keepdims=True)
    logit_full = (gate_of * (grad_of - weighted)).astype(bf16)
    got_back, logit_full, mix, router_wide = lax.optimization_barrier(
        (got_back, logit_full, mix, router_wide)
    )

    residual_grad, bands, small = finish(
        mix, got_back, pre_norm, out_grad, gain, logit_full, router_wide, normed, lax.axis_size("y")
    )

    square, small = gather_square(bands, small)
    context_grad, weight_grad, small = ring_scatter(
        square,
        (
            (functools.partial(projection, context_kernel, "context_part"), weight_band, "y"),
            (functools.partial(projection, weight_kernel, "weight_part"), context_band, "x"),
        ),
        small,
    )
    router_grad = small[:experts].T
    gain_grad = small[experts]
    return (residual_grad, gate_grad, router_grad, gain_grad, context_grad, weight_grad)


def solution(mesh):
    devices = np.asarray(mesh.devices)
    fine = Mesh(devices.reshape(4, 4, 4, 2), EVERY)
    rows = P(EVERY, None)
    cube = P(EVERY, None, None)
    split = P(DP, TENSOR)
    return jax.shard_map(
        shards,
        mesh=fine,
        in_specs=(rows, rows, rows, rows, P(), P(), cube, cube, cube, split, split),
        out_specs=(rows, rows, P(TENSOR, None), P(TENSOR), split, split),
        check_vma=False,
    )
```

```python
import functools

import jax
import jax.numpy as jnp
import numpy as np
from jax import lax
from jax.experimental import pallas as pl
from jax.experimental.pallas import tpu as pltpu
from jax.sharding import Mesh, PartitionSpec as P

CHIP = ("y", "x", "z")
EVERY = ("y", "x", "z", "core")
DP = ("y", "x")
TENSOR = ("z", "core")
SWAP = [(0, 1), (1, 0)]
WIDE = 512
SOME = 8
MIB = 1024 * 1024
bf16 = jnp.bfloat16
f32 = jnp.float32
OVER_ROWS = (((0,), (0,)), ((), ()))
OVER_LAST = (((1,), (1,)), ((), ()))


def swap_cores(value):
    return lax.ppermute(value, "core", SWAP)


def exchange(value, axes):
    return lax.all_to_all(value, axes, split_axis=0, concat_axis=0, tiled=True)


def cross_sum(value, axis):
    size = lax.axis_size(axis)
    value = value.astype(bf16)
    one, two, three = [
        lax.ppermute(value, axis, [(i, i ^ mask) for i in range(size)]) for mask in (1, 2, 3)
    ]
    return (value.astype(f32) + two.astype(f32)) + (one.astype(f32) + three.astype(f32))


def shift(value, axis, step):
    size = lax.axis_size(axis)
    return lax.ppermute(value, axis, [(i, (i + step) % size) for i in range(size)])


def pass_on_kernel(*refs):
    ins, outs = refs[: len(refs) * 2 // 3], refs[len(refs) * 2 // 3 :]
    for at, out in enumerate(outs):
        here, came = ins[2 * at], ins[2 * at + 1]
        half = here.shape[0]
        first = (at % 2) * half
        came = came[first : first + half, :]
        out[...] = (here[...].astype(f32) + came.astype(f32)).astype(bf16)


def close_kernel(*refs):
    ins, outs = refs[:-2], refs[-2:]
    for at, out in enumerate(outs):
        upper, lower, from_left, from_right, last_left, last_right = ins[6 * at : 6 * at + 6]
        half = upper.shape[0]
        out[:half, :] = (
            upper[...].astype(f32) + from_right[:half, :].astype(f32) + last_left[...].astype(f32)
        ).astype(bf16)
        out[half:, :] = (
            lower[...].astype(f32) + from_left[half:, :].astype(f32) + last_right[...].astype(f32)
        ).astype(bf16)


def whole_call(kernel, name, shapes, *arrays):
    whole = pl.BlockSpec(memory_space=pltpu.VMEM)
    return pl.pallas_call(
        kernel,
        in_specs=[whole] * len(arrays),
        out_specs=tuple(whole for _ in shapes),
        out_shape=tuple(jax.ShapeDtypeStruct(shape, bf16) for shape in shapes),
        compiler_params=params(0, 16),
        name=name,
    )(*arrays)


def ring_scatter(square, rings, small):
    places = [lax.axis_index(axis).astype(jnp.int32).reshape(1) for _, _, axis in rings]
    firsts = [
        kernel(place, square, band, (((2, 0), (1, 1)), ((3, 0), (2, 1))))
        for place, (kernel, band, _) in zip(places, rings)
    ]
    firsts, small = lax.optimization_barrier((firsts, small))
    sent = [
        (shift(to_right, axis, 1), shift(to_left, axis, -1))
        for (to_right, to_left), (_, _, axis) in zip(firsts, rings)
    ]
    rests = [
        kernel(place, square, band, (((1, 0),), ((3, 1),), ((0, 0),), ((0, 1),)))
        for place, (kernel, band, _) in zip(places, rings)
    ]
    sent, rests = lax.optimization_barrier((sent, rests))
    half, width = rests[0][0].shape
    passed = whole_call(
        pass_on_kernel,
        "pass_on",
        [(half, width)] * 4,
        *[
            v
            for came, rest in zip(sent, rests)
            for v in (rest[0], *outside(came[0]), rest[1], *outside(came[1]))
        ],
    )
    last = []
    for at, (_, _, axis) in enumerate(rings):
        last.append((shift(passed[2 * at], axis, 1), shift(passed[2 * at + 1], axis, -1)))
    sums = whole_call(
        close_kernel,
        "close",
        [(2 * half, width)] * 2,
        *[
            v
            for came, rest, end in zip(sent, rests, last)
            for v in (rest[2], rest[3], *outside(*came, *end))
        ],
    )
    return (*sums, small)


def gather_kernel(place_ref, *refs):
    *pieces, out_ref, sems = refs
    sides, tok_rows, _ = pieces[0].shape
    y, z, core = place_ref[0], place_ref[1], place_ref[2]
    copies = []
    for at, piece in enumerate(pieces):
        side, turn = at // sides, at % sides
        here = lax.rem(z - turn + sides, sides) * 2 + (core if side == 0 else 1 - core)
        rows = pl.ds(pl.multiple_of(here * tok_rows, tok_rows), tok_rows)
        for back in range(sides):
            copies.append(
                pltpu.make_async_copy(
                    piece.at[back],
                    out_ref.at[lax.rem(y - back + sides, sides), rows],
                    sems.at[at * sides + back],
                )
            )
    for copy in copies:
        copy.start()
    for copy in copies:
        copy.wait()


def gather_square(bands, small):
    sides, tok_rows, width = bands.shape
    y, z, core = lax.axis_index("y"), lax.axis_index("z"), lax.axis_index("core")

    def block(value, index):
        return lax.dynamic_index_in_dim(value, index, 0, keepdims=False)

    own = block(bands, y)
    piece = [own] + [
        shift(block(bands, lax.rem(y + step, sides)), "y", step) for step in range(1, sides)
    ]
    small = small.reshape(sides, 2, *small.shape[1:])
    mine = lax.dynamic_index_in_dim(small, core, 1, keepdims=False)
    theirs = lax.dynamic_index_in_dim(small, 1 - core, 1, keepdims=False)
    small = mine + swap_cores(theirs.astype(bf16)).astype(f32)
    piece = jnp.stack(piece)
    piece, small = lax.optimization_barrier((piece, small))
    passed = small.astype(bf16)
    came = [
        shift(block(passed, lax.rem(z + step, sides)), "z", step) for step in range(1, sides)
    ]
    near = [piece] + [shift(piece, "z", step) for step in (1, 3, 2)]
    far = [swap_cores(p) for p in near]
    small = block(small, z) + sum(c.astype(f32) for c in came)
    small = cross_sum(small, "x")
    near, far, small = lax.optimization_barrier((near, far, small))
    small = cross_sum(small, "y")
    near = [near[0], near[1], near[3], near[2]]
    far = [far[0], far[1], far[3], far[2]]
    whole = pl.BlockSpec(memory_space=pltpu.VMEM)
    square = pl.pallas_call(
        gather_kernel,
        in_specs=[pl.BlockSpec(memory_space=pltpu.SMEM)]
        + [pl.BlockSpec(memory_space=pl.ANY)] * (2 * sides),
        out_specs=whole,
        out_shape=jax.ShapeDtypeStruct((sides, 2 * sides * tok_rows, width), bf16),
        scratch_shapes=[pltpu.SemaphoreType.DMA((2 * sides * sides,))],
        compiler_params=params(0, 16),
        name="gather_square",
    )(jnp.stack([y, z, core]).astype(jnp.int32), *near, *far)
    return square, small


def context_kernel(wanted, place_ref, square_ref, band_ref, *out_refs):
    sides, tokens, _ = square_ref.shape
    half = tokens // 2
    for blocks, out_ref in zip(wanted, out_refs):
        for at, (step, part) in enumerate(blocks):
            block = lax.rem(place_ref[0] + step, sides)
            rows = square_ref[pl.ds(block, 1), part * half : (part + 1) * half, :][0]
            out_ref[at * half : (at + 1) * half, :] = jnp.dot(
                rows, band_ref[...], preferred_element_type=f32
            ).astype(bf16)


def weight_kernel(wanted, place_ref, square_ref, band_ref, *out_refs):
    sides, tokens, depth = square_ref.shape
    half = depth // sides // 2
    for blocks, out_ref in zip(wanted, out_refs):
        for at, (step, part) in enumerate(blocks):
            block = lax.rem(place_ref[0] + step, sides)
            columns = pl.ds(pl.multiple_of((2 * block + part) * half, half), half)
            out_ref[at * half : (at + 1) * half, :] = lax.dot_general(
                square_ref[:, :, columns].reshape(sides * tokens, half),
                band_ref[...],
                OVER_ROWS,
                preferred_element_type=f32,
            ).astype(bf16)


def projection(kernel, name, place, square, band, wanted):
    width = band.shape[1]
    half = square.shape[1] // 2
    count = sum(len(blocks) for blocks in wanted)
    whole = pl.BlockSpec(memory_space=pltpu.VMEM)
    return pl.pallas_call(
        functools.partial(kernel, wanted),
        in_specs=[pl.BlockSpec(memory_space=pltpu.SMEM), whole, whole],
        out_specs=tuple(whole for _ in wanted),
        out_shape=tuple(
            jax.ShapeDtypeStruct((half * len(blocks), width), bf16) for blocks in wanted
        ),
        compiler_params=params(0, 16),
        cost_estimate=pl.CostEstimate(
            flops=2 * half * count * band.shape[0] * width,
            bytes_accessed=5_000_000,
            transcendentals=0,
        ),
        name=name,
    )(place, square, *kept(band))


def kept(*arrays):
    return [pltpu.with_memory_space_constraint(a, pltpu.VMEM) for a in arrays]


def outside(*arrays):
    return [pltpu.with_memory_space_constraint(a, pltpu.HBM) for a in arrays]


def params(grid=0, mib=16):
    return pltpu.CompilerParams(
        vmem_limit_bytes=mib * MIB,
        dimension_semantics=("arbitrary",) * grid if grid else None,
    )


def slot_codes(routes_wide, experts, pieces, tok_rows):
    columns = pieces * tok_rows
    expert = lax.broadcasted_iota(jnp.int32, (experts, columns), 0)
    named = expert == routes_wide[0:1, :]
    for choice in range(1, routes_wide.shape[0]):
        named = named | (expert == routes_wide[choice : choice + 1, :])
    before = lax.broadcasted_iota(jnp.int32, (columns, columns), 0)
    after = lax.broadcasted_iota(jnp.int32, (columns, columns), 1)
    earlier = (before // tok_rows == after // tok_rows) & (before < after)
    rank = jnp.dot(
        jnp.where(named, 1.0, 0.0).astype(bf16),
        jnp.where(earlier, 1.0, 0.0).astype(bf16),
        preferred_element_type=f32,
    )
    piece = (lax.broadcasted_iota(jnp.int32, (experts, columns), 1) // tok_rows).astype(f32)
    return jnp.where(named, piece * 8.0 + rank, -1.0)


def row_codes(shape, capacity, block, dim):
    row = lax.broadcasted_iota(jnp.int32, shape, dim) % block
    return ((row // capacity) * 8 + row % capacity).astype(f32)


def place_kernel(
    capacity, pre_ref, grad_ref, gain_ref, routes_ref, send_ref, code_ref, normed_ref, source
):
    tok_rows, features = pre_ref.shape
    experts, columns = code_ref.shape
    pieces = features // WIDE
    block = pieces * capacity
    group = pl.program_id(0)
    some = send_ref.shape[0]
    rows = some * block

    @pl.when(group == 0)
    def prepare():
        hidden = pre_ref[...].astype(f32)
        inverse = lax.rsqrt(jnp.mean(hidden * hidden, axis=-1, keepdims=True) + 1e-06)
        normed = (hidden * inverse * gain_ref[...]).astype(bf16)
        normed_ref[...] = normed
        for piece in range(pieces):
            at = pl.ds(piece * tok_rows, tok_rows)
            source[at, :WIDE] = normed[:, piece * WIDE : (piece + 1) * WIDE]
            source[at, WIDE:] = grad_ref[:, piece * WIDE : (piece + 1) * WIDE]
        code_ref[...] = slot_codes(routes_ref[...], experts, pieces, tok_rows)

    code = code_ref[pl.ds(pl.multiple_of(group * some, some), some), :]
    want = row_codes((some, block, columns), capacity, block, 1)
    hit = jnp.where(code[:, None, :] == want, 1.0, 0.0).astype(bf16).reshape(rows, columns)
    moved = jnp.dot(hit, source[...], preferred_element_type=f32).astype(bf16)
    send_ref[:, :block, :] = moved[:, :WIDE].reshape(some, block, WIDE)
    send_ref[:, block:, :] = moved[:, WIDE:].reshape(some, block, WIDE)


def place(pre_norm, out_grad, norm_gain, routes_wide, experts, capacity):
    tok_rows, features = pre_norm.shape
    pieces = features // WIDE
    block = pieces * capacity
    some = 8
    columns = pieces * tok_rows

    def whole(*shape):
        return pl.BlockSpec(shape, lambda i: (0,) * len(shape))

    return pl.pallas_call(
        functools.partial(place_kernel, capacity),
        grid=(experts // some,),
        in_specs=[
            whole(tok_rows, features),
            whole(tok_rows, features),
            whole(1, features),
            whole(*routes_wide.shape),
        ],
        out_specs=(
            pl.BlockSpec((some, 2 * block, WIDE), lambda i: (i, 0, 0)),
            whole(experts, columns),
            whole(tok_rows, features),
        ),
        out_shape=(
            pltpu.HBM((experts, 2 * block, WIDE), bf16),
            jax.ShapeDtypeStruct((experts, columns), f32),
            jax.ShapeDtypeStruct((tok_rows, features), bf16),
        ),
        scratch_shapes=[pltpu.VMEM((columns, 2 * WIDE), bf16)],
        compiler_params=params(1, 16),
        name="place",
    )(*outside(pre_norm, out_grad, norm_gain), routes_wide)


def order_matrix(capacity, block):
    at = np.arange(SOME * block)
    moved = (at % block) // capacity * (SOME * capacity) + at // block * capacity + at % capacity
    return jnp.asarray(moved[None, :] == at[:, None], bf16)


def spread_kernel(capacity, got_ref, order_ref, rows_ref):
    some, block, _ = got_ref.shape
    pieces = block // capacity
    span = SOME * capacity
    for group in range(some // SOME):
        source = got_ref[group * SOME : (group + 1) * SOME].reshape(SOME * block, WIDE)
        moved = jnp.dot(order_ref[...], source, preferred_element_type=f32).astype(bf16)
        for piece in range(pieces):
            rows_ref[group * span : (group + 1) * span, piece * WIDE : (piece + 1) * WIDE] = moved[
                piece * span : (piece + 1) * span
            ]


def spread(got, kind, order, capacity):
    sources, double, _ = got.shape
    block = double // 2
    features = block // capacity * WIDE
    some = 2 * SOME
    return pl.pallas_call(
        functools.partial(spread_kernel, capacity),
        grid=(sources // some,),
        in_specs=[
            pl.BlockSpec((some, block, WIDE), lambda i: (i, kind, 0)),
            pl.BlockSpec(order.shape, lambda i: (0, 0)),
        ],
        out_specs=pl.BlockSpec((some * capacity, features), lambda i: (i, 0)),
        out_shape=jax.ShapeDtypeStruct((sources * capacity, features), bf16),
        compiler_params=params(1),
        name="spread",
    )(got, order)


def forward_kernel(own_ref, other_ref, gate_ref, up_ref, gate_pre_ref, up_pre_ref):
    count = own_ref.shape[0]
    units = gate_ref.shape[2]
    tile = 256
    for mat, out in ((gate_ref, gate_pre_ref), (up_ref, up_pre_ref)):
        for n in range(units // tile):
            at = slice(n * tile, (n + 1) * tile)
            out[:count, at] = jnp.dot(own_ref[...], mat[0, :, at], preferred_element_type=f32)
            out[count:, at] = jnp.dot(other_ref[...], mat[0, :, at], preferred_element_type=f32)


def forward(own, other, w_gate, w_up):
    count, features = own.shape
    units = w_gate.shape[2]
    inside = pl.BlockSpec(memory_space=pltpu.VMEM)
    return pl.pallas_call(
        forward_kernel,
        in_specs=[inside] * 4,
        out_specs=(inside, inside),
        out_shape=(jax.ShapeDtypeStruct((2 * count, units), f32),) * 2,
        compiler_params=params(0, 10),
        cost_estimate=pl.CostEstimate(
            flops=8 * count * features * units, bytes_accessed=24_000_000, transcendentals=0
        ),
        name="forward",
    )(own, other, *kept(w_gate, w_up))


def hidden_kernel(
    capacity, own_ref, other_ref, down_ref, gate_pre_ref, up_pre_ref, gg_ref, gu_ref, *part_refs
):
    count = own_ref.shape[0]
    units = down_ref.shape[1]
    tile = 256
    for half, rows in enumerate((own_ref, other_ref)):
        here = slice(half * count, (half + 1) * count)
        part = jnp.zeros((count, 1), f32)
        for n in range(units // tile):
            at = slice(n * tile, (n + 1) * tile)
            upstream = lax.dot_general(
                rows[...], down_ref[0, at, :], OVER_LAST, preferred_element_type=f32
            )
            gate_pre = gate_pre_ref[here, at]
            up_pre = up_pre_ref[here, at]
            sig = jax.nn.sigmoid(gate_pre)
            grad_up = upstream * (gate_pre * sig)
            part = part + jnp.sum(grad_up * up_pre, axis=-1, keepdims=True)
            gu_ref[here, at] = grad_up.astype(bf16)
            gg_ref[here, at] = (
                upstream * up_pre * sig * (1.0 + gate_pre * (1.0 - sig))
            ).astype(bf16)
        part_rows = part_refs[half].shape[0]
        rows_of = lax.broadcasted_iota(jnp.int32, (part_rows, count), 0)
        slots_of = lax.broadcasted_iota(jnp.int32, (part_rows, count), 1)
        same = (rows_of // 8 == slots_of // capacity) & (rows_of % 8 == slots_of % capacity)
        part_refs[half][...] = jnp.dot(
            jnp.where(same, 1.0, 0.0).astype(bf16),
            jnp.broadcast_to(part.astype(bf16), (count, 128)),
            preferred_element_type=f32,
        )


def hidden_grads(own, other, w_down, gate_pre, up_pre, capacity):
    count, features = own.shape
    units = w_down.shape[1]
    inside = pl.BlockSpec(memory_space=pltpu.VMEM)
    return pl.pallas_call(
        functools.partial(hidden_kernel, capacity),
        in_specs=[inside] * 5,
        out_specs=(inside,) * 4,
        out_shape=(
            jax.ShapeDtypeStruct((2 * count, units), bf16),
            jax.ShapeDtypeStruct((2 * count, units), bf16),
            jax.ShapeDtypeStruct((count // capacity * 8, 128), f32),
            jax.ShapeDtypeStruct((count // capacity * 8, 128), f32),
        ),
        compiler_params=params(0, 10),
        cost_estimate=pl.CostEstimate(
            flops=4 * count * features * units, bytes_accessed=24_000_000, transcendentals=0
        ),
        name="hidden_grads",
    )(*outside(own, other), *kept(w_down), gate_pre, up_pre)


def term_kernel(gg_ref, gu_ref, gate_ref, up_ref, own_ref, other_ref):
    count, features = own_ref.shape
    tile = 512
    for n in range(features // tile):
        at = slice(n * tile, (n + 1) * tile)
        term = lax.dot_general(
            gg_ref[...], gate_ref[0, at, :], OVER_LAST, preferred_element_type=f32
        )
        term = term + lax.dot_general(
            gu_ref[...], up_ref[0, at, :], OVER_LAST, preferred_element_type=f32
        )
        term = term.astype(bf16)
        own_ref[:, at] = term[:count]
        other_ref[:, at] = term[count:]


def terms(grad_gate, grad_up, w_gate, w_up):
    count = grad_gate.shape[0] // 2
    units = grad_gate.shape[1]
    features = w_gate.shape[1]
    inside = pl.BlockSpec(memory_space=pltpu.VMEM)
    return pl.pallas_call(
        term_kernel,
        in_specs=[inside] * 4,
        out_specs=(inside, inside),
        out_shape=(jax.ShapeDtypeStruct((count, features), bf16),) * 2,
        compiler_params=params(0, 10),
        cost_estimate=pl.CostEstimate(
            flops=8 * count * features * units, bytes_accessed=17_000_000, transcendentals=0
        ),
        name="terms",
    )(grad_gate, grad_up, *kept(w_gate, w_up))


def pack_kernel(
    capacity, own_ref, other_ref, order_ref, own_part_ref, other_part_ref, chip_ref, send_ref, held
):
    rows, features = own_ref.shape
    pieces = features // WIDE
    span = SOME * capacity
    block = pieces * capacity
    for group in range(rows // span):
        here = slice(group * span, (group + 1) * span)
        for piece in range(pieces):
            at = slice(piece * WIDE, (piece + 1) * WIDE)
            held[group, pl.ds(piece * span, span), :] = (
                own_ref[here, at].astype(f32) + other_ref[here, at].astype(f32)
            ).astype(bf16)
        moved = lax.dot_general(
            order_ref[...], held[group], OVER_ROWS, preferred_element_type=f32
        )
        send_ref[group * SOME : (group + 1) * SOME, :block, :] = moved.astype(bf16).reshape(
            SOME, block, WIDE
        )
    part = own_part_ref[...] + other_part_ref[...]
    high = part.astype(bf16).astype(f32)
    lane = lax.broadcasted_iota(jnp.int32, part.shape, 1)
    half = part.shape[1] // 2
    part = jnp.where(lane < half, high, part - high)
    part = jnp.where(lane % half == chip_ref[0], part, 0.0)
    part = part.reshape(send_ref.shape[0], 8, part.shape[1])
    part = jnp.concatenate(
        [part, jnp.zeros((*part.shape[:2], WIDE - part.shape[2]), f32)], axis=2
    )
    send_ref[:, block:, :] = part.astype(bf16)


def pack(own, other, order, capacity, own_part, other_part):
    count, features = own.shape
    block = features // WIDE * capacity
    groups = 2
    span = groups * SOME * capacity
    chip = lax.axis_index(CHIP).astype(jnp.int32).reshape(1)
    return pl.pallas_call(
        functools.partial(pack_kernel, capacity),
        grid=(count // span,),
        in_specs=[
            pl.BlockSpec((span, features), lambda i: (i, 0)),
            pl.BlockSpec((span, features), lambda i: (i, 0)),
            pl.BlockSpec(order.shape, lambda i: (0, 0)),
            pl.BlockSpec((groups * SOME * 8, 128), lambda i: (i, 0)),
            pl.BlockSpec((groups * SOME * 8, 128), lambda i: (i, 0)),
            pl.BlockSpec(memory_space=pltpu.SMEM),
        ],
        out_specs=pl.BlockSpec((groups * SOME, block + 8, WIDE), lambda i: (i, 0, 0)),
        out_shape=pltpu.HBM((count // capacity, block + 8, WIDE), bf16),
        scratch_shapes=[pltpu.VMEM((groups, SOME * block, WIDE), bf16)],
        compiler_params=params(1),
        name="pack",
    )(own, other, order, own_part, other_part, chip)


def mix_kernel(capacity, code_ref, gate_ref, mix_ref):
    some, columns = code_ref.shape
    rows = mix_ref.shape[1]
    block = rows // some
    want = row_codes((some, block, columns), capacity, block, 1)
    mixing = jnp.where(code_ref[...][:, None, :] == want, gate_ref[...][:, None, :], 0.0)
    mixing = mixing.reshape(rows, columns)
    high = mixing.astype(bf16)
    low = (mixing - high.astype(f32)).astype(bf16)
    mix_ref[:columns, :] = high.T
    mix_ref[columns:, :] = low.T


def mixings(code, gate_wide, capacity, block):
    experts, columns = code.shape
    some = 8
    return pl.pallas_call(
        functools.partial(mix_kernel, capacity),
        grid=(experts // some,),
        in_specs=[
            pl.BlockSpec((some, columns), lambda i: (i, 0)),
            pl.BlockSpec((some, columns), lambda i: (i, 0)),
        ],
        out_specs=pl.BlockSpec((2 * columns, some * block), lambda i: (0, i)),
        out_shape=jax.ShapeDtypeStruct((2 * columns, experts * block), bf16),
        compiler_params=params(1),
        name="mixings",
    )(code, gate_wide)


def finish_kernel(
    mix_ref, back_ref, pre_ref, grad_ref, gain_ref, router_ref, normed_ref,
    code_ref, gate_ref, routes_ref,
    residual_ref, bands_ref, small_ref, gate_grad_ref,
):
    tok_rows, features = pre_ref.shape
    columns = mix_ref.shape[0] // 2
    pieces = features // WIDE
    experts, rows, _ = back_ref.shape
    block = rows - 8
    both = jnp.dot(
        mix_ref[...],
        back_ref[:, :block, :].reshape(experts * block, WIDE),
        preferred_element_type=f32,
    )
    slot = lax.broadcasted_iota(jnp.int32, (experts, 8, tok_rows), 1).astype(f32)
    hit = jnp.where(code_ref[:, :tok_rows][:, None, :] == slot, 1.0, 0.0)
    part = back_ref[:, block:, :128].astype(f32).reshape(experts * 8, 128).astype(bf16)
    part = lax.dot_general(
        hit.reshape(experts * 8, tok_rows).astype(bf16), part, OVER_ROWS,
        preferred_element_type=f32,
    )
    grad_of = part[:, :experts] + part[:, experts:]
    expert = lax.broadcasted_iota(jnp.int32, (tok_rows, experts), 1)
    for choice in range(routes_ref.shape[1]):
        named = expert == routes_ref[:, choice : choice + 1]
        gate_grad_ref[:, choice : choice + 1] = jnp.sum(
            jnp.where(named, grad_of, 0.0), axis=-1, keepdims=True
        )
    gate_of = gate_ref[...]
    weighted = jnp.sum(gate_of * grad_of, axis=-1, keepdims=True)
    logit_full = (gate_of * (grad_of - weighted)).astype(bf16)
    expert_grad = both[:columns] + both[columns:]
    hidden = pre_ref[...].astype(f32)
    inverse = lax.rsqrt(jnp.mean(hidden * hidden, axis=-1, keepdims=True) + 1e-06)
    router_term = jnp.dot(logit_full, router_ref[...], preferred_element_type=f32)
    router_part = lax.dot_general(
        logit_full, normed_ref[...], OVER_ROWS, preferred_element_type=f32
    )
    spare = small_ref.shape[1] - experts
    per_band = bands_ref.shape[2] // WIDE
    moment = jnp.zeros((tok_rows, 1), f32)
    normed_grads = []
    for piece in range(pieces):
        at = slice(piece * WIDE, (piece + 1) * WIDE)
        normed_grad = (
            expert_grad[piece * tok_rows : (piece + 1) * tok_rows] + router_term[:, at]
        )
        normed_grads.append(normed_grad)
        small_ref[piece, :experts, :] = router_part[:, at]
        small_ref[piece, experts:, :] = jnp.broadcast_to(
            jnp.sum(normed_grad * hidden[:, at] * inverse, axis=0, keepdims=True), (spare, WIDE)
        )
        moment = moment + jnp.sum(
            hidden[:, at] * gain_ref[:, at] * normed_grad, axis=-1, keepdims=True
        )
    factor = inverse * inverse * inverse * (moment / features)
    for piece in range(pieces):
        at = slice(piece * WIDE, (piece + 1) * WIDE)
        residual = (
            grad_ref[:, at].astype(f32)
            + inverse * gain_ref[:, at] * normed_grads[piece]
            - hidden[:, at] * factor
        ).astype(bf16)
        residual_ref[:, at] = residual
        inner = piece % per_band * WIDE
        bands_ref[piece // per_band, :, inner : inner + WIDE] = residual


def finish(
    mix, back, pre_norm, out_grad, norm_gain, router_wide, normed, code, gate_of, routes, bands
):
    tok_rows, features = pre_norm.shape
    experts = gate_of.shape[1]
    return pl.pallas_call(
        finish_kernel,
        out_shape=(
            jax.ShapeDtypeStruct((tok_rows, features), bf16),
            jax.ShapeDtypeStruct((bands, tok_rows, features // bands), bf16),
            jax.ShapeDtypeStruct((features // WIDE, experts + 8, WIDE), f32),
            jax.ShapeDtypeStruct(routes.shape, f32),
        ),
        compiler_params=params(0, 24),
        name="finish",
    )(
        mix,
        *outside(back, pre_norm, out_grad, norm_gain),
        router_wide,
        *outside(normed),
        code,
        gate_of,
        routes,
    )


def shards(
    pre_norm,
    out_grad,
    routes,
    gate_probs,
    norm_gain,
    router_weight,
    w_gate,
    w_up,
    w_down,
    context,
    out_weight,
):
    tok_rows, features = pre_norm.shape
    top = routes.shape[1]
    experts = router_weight.shape[1]
    capacity = tok_rows * top * 3 // (2 * experts)
    pieces = features // WIDE
    block = pieces * capacity
    gain = norm_gain.reshape(1, features)

    routes_wide = jnp.tile(routes.T, (1, pieces))
    send, code, normed = place(pre_norm, out_grad, gain, routes_wide, experts, capacity)

    got = exchange(send, CHIP)

    order = order_matrix(capacity, block)
    got, code, normed, out_weight, context, routes, gate_probs = lax.optimization_barrier(
        (got, code, normed, out_weight, context, routes, gate_probs)
    )

    weight_band = lax.all_gather(out_weight, "x", axis=0, tiled=True)
    context_band = lax.all_gather(context, "y", axis=0, tiled=True)

    own_tokens = spread(got, 0, order, capacity)
    other_tokens = swap_cores(own_tokens)
    own_grads = spread(got, 1, order, capacity)
    other_grads = swap_cores(own_grads)
    gate_pre, up_pre = forward(own_tokens, other_tokens, w_gate, w_up)
    grad_gate, grad_up, own_part, other_part = hidden_grads(
        own_grads, other_grads, w_down, gate_pre, up_pre, capacity
    )
    other_part = swap_cores(other_part)
    own_term, other_term = terms(grad_gate, grad_up, w_gate, w_up)
    other_term = swap_cores(other_term)
    other_term, weight_band, context_band = lax.optimization_barrier(
        (other_term, weight_band, context_band)
    )
    send_back = pack(own_term, other_term, order, capacity, own_part, other_part)
    send_back, code, routes, gate_probs, router_weight = lax.optimization_barrier(
        (send_back, code, routes, gate_probs, router_weight)
    )
    got_back = exchange(send_back, CHIP)

    named = routes[:, :, None] == jnp.arange(experts, dtype=jnp.int32)[None, None, :]
    gate_of = jnp.sum(jnp.where(named, gate_probs[:, :, None], 0.0), axis=1)
    mix = mixings(code, jnp.tile(gate_of.T, (1, pieces)), capacity, block)
    router_wide = router_weight.T

    got_back, mix, router_wide, gate_of = lax.optimization_barrier(
        (got_back, mix, router_wide, gate_of)
    )
    residual_grad, bands, small, gate_grad = finish(
        mix, got_back, pre_norm, out_grad, gain, router_wide, normed, code, gate_of, routes,
        lax.axis_size("y"),
    )

    square, small = gather_square(bands, small)
    context_grad, weight_grad, small = ring_scatter(
        square,
        (
            (functools.partial(projection, context_kernel, "context_part"), weight_band, "y"),
            (functools.partial(projection, weight_kernel, "weight_part"), context_band, "x"),
        ),
        small,
    )
    router_grad = small[:experts].T
    gain_grad = small[experts]
    return (residual_grad, gate_grad, router_grad, gain_grad, context_grad, weight_grad)


def solution(mesh):
    devices = np.asarray(mesh.devices)
    fine = Mesh(devices.reshape(4, 4, 4, 2), EVERY)
    rows = P(EVERY, None)
    cube = P(EVERY, None, None)
    split = P(DP, TENSOR)
    return jax.shard_map(
        shards,
        mesh=fine,
        in_specs=(rows, rows, rows, rows, P(), P(), cube, cube, cube, split, split),
        out_specs=(rows, rows, P(TENSOR, None), P(TENSOR), split, split),
        check_vma=False,
    )
```

```python
import functools

import jax
import jax.numpy as jnp
import numpy as np
from jax import lax
from jax.experimental import pallas as pl
from jax.experimental.pallas import tpu as pltpu
from jax.sharding import Mesh, PartitionSpec as P

CHIP = ("y", "x", "z")
EVERY = ("y", "x", "z", "core")
DP = ("y", "x")
TENSOR = ("z", "core")
SWAP = [(0, 1), (1, 0)]
WIDE = 512
SOME = 8
MIB = 1024 * 1024
bf16 = jnp.bfloat16
f32 = jnp.float32
OVER_ROWS = (((0,), (0,)), ((), ()))
OVER_LAST = (((1,), (1,)), ((), ()))


def swap_cores(value):
    return lax.ppermute(value, "core", SWAP)


def exchange(value, axes):
    return lax.all_to_all(value, axes, split_axis=0, concat_axis=0, tiled=True)


def cross_sum(value, axis):
    size = lax.axis_size(axis)
    value = value.astype(bf16)
    one, two, three = [
        lax.ppermute(value, axis, [(i, i ^ mask) for i in range(size)]) for mask in (1, 2, 3)
    ]
    return (value.astype(f32) + two.astype(f32)) + (one.astype(f32) + three.astype(f32))


def shift(value, axis, step):
    size = lax.axis_size(axis)
    return lax.ppermute(value, axis, [(i, (i + step) % size) for i in range(size)])


def pass_on_kernel(*refs):
    ins, outs = refs[: len(refs) * 2 // 3], refs[len(refs) * 2 // 3 :]
    for at, out in enumerate(outs):
        here, came = ins[2 * at], ins[2 * at + 1]
        half = here.shape[0]
        first = (at % 2) * half
        came = came[first : first + half, :]
        out[...] = (here[...].astype(f32) + came.astype(f32)).astype(bf16)


def close_kernel(*refs):
    ins, outs = refs[:-2], refs[-2:]
    for at, out in enumerate(outs):
        upper, lower, from_left, from_right, last_left, last_right = ins[6 * at : 6 * at + 6]
        half = upper.shape[0]
        out[:half, :] = (
            upper[...].astype(f32) + from_right[:half, :].astype(f32) + last_left[...].astype(f32)
        ).astype(bf16)
        out[half:, :] = (
            lower[...].astype(f32) + from_left[half:, :].astype(f32) + last_right[...].astype(f32)
        ).astype(bf16)


def whole_call(kernel, name, shapes, *arrays):
    whole = pl.BlockSpec(memory_space=pltpu.VMEM)
    return pl.pallas_call(
        kernel,
        in_specs=[whole] * len(arrays),
        out_specs=tuple(whole for _ in shapes),
        out_shape=tuple(jax.ShapeDtypeStruct(shape, bf16) for shape in shapes),
        compiler_params=params(0, 16),
        name=name,
    )(*arrays)


def ring_scatter(square, rings, small):
    places = [lax.axis_index(axis).astype(jnp.int32).reshape(1) for _, _, axis in rings]
    firsts = [
        kernel(place, square, band, (((2, 0), (1, 1)), ((3, 0), (2, 1))))
        for place, (kernel, band, _) in zip(places, rings)
    ]
    firsts, small = lax.optimization_barrier((firsts, small))
    sent = [
        (shift(to_right, axis, 1), shift(to_left, axis, -1))
        for (to_right, to_left), (_, _, axis) in zip(firsts, rings)
    ]
    rests = [
        kernel(place, square, band, (((1, 0),), ((3, 1),), ((0, 0),), ((0, 1),)))
        for place, (kernel, band, _) in zip(places, rings)
    ]
    half, width = rests[0][0].shape
    passed = whole_call(
        pass_on_kernel,
        "pass_on",
        [(half, width)] * 4,
        *[
            v
            for came, rest in zip(sent, rests)
            for v in (rest[0], *outside(came[0]), rest[1], *outside(came[1]))
        ],
    )
    last = []
    for at, (_, _, axis) in enumerate(rings):
        last.append((shift(passed[2 * at], axis, 1), shift(passed[2 * at + 1], axis, -1)))
    sums = whole_call(
        close_kernel,
        "close",
        [(2 * half, width)] * 2,
        *[
            v
            for came, rest, end in zip(sent, rests, last)
            for v in (rest[2], rest[3], *outside(*came, *end))
        ],
    )
    return (*sums, small)


def gather_kernel(place_ref, *refs):
    *pieces, out_ref, sems = refs
    sides, tok_rows, _ = pieces[0].shape
    y, z, core = place_ref[0], place_ref[1], place_ref[2]
    copies = []
    for at, piece in enumerate(pieces):
        side, turn = at // sides, at % sides
        here = lax.rem(z - turn + sides, sides) * 2 + (core if side == 0 else 1 - core)
        rows = pl.ds(pl.multiple_of(here * tok_rows, tok_rows), tok_rows)
        for back in range(sides):
            copies.append(
                pltpu.make_async_copy(
                    piece.at[back],
                    out_ref.at[lax.rem(y - back + sides, sides), rows],
                    sems.at[at * sides + back],
                )
            )
    for copy in copies:
        copy.start()
    for copy in copies:
        copy.wait()


def gather_square(bands, small):
    sides, tok_rows, width = bands.shape
    y, z, core = lax.axis_index("y"), lax.axis_index("z"), lax.axis_index("core")

    def block(value, index):
        return lax.dynamic_index_in_dim(value, index, 0, keepdims=False)

    own = block(bands, y)
    piece = [own] + [
        shift(block(bands, lax.rem(y + step, sides)), "y", step) for step in range(1, sides)
    ]
    small = small.reshape(sides, 2, *small.shape[1:])
    mine = lax.dynamic_index_in_dim(small, core, 1, keepdims=False)
    theirs = lax.dynamic_index_in_dim(small, 1 - core, 1, keepdims=False)
    small = mine + swap_cores(theirs.astype(bf16)).astype(f32)
    piece = jnp.stack(piece)
    piece, small = lax.optimization_barrier((piece, small))
    passed = small.astype(bf16)
    came = [
        shift(block(passed, lax.rem(z + step, sides)), "z", step) for step in range(1, sides)
    ]
    near = [piece] + [shift(piece, "z", step) for step in (1, 3, 2)]
    far = [swap_cores(p) for p in near]
    small = block(small, z) + sum(c.astype(f32) for c in came)
    small = cross_sum(small, "x")
    near, far, small = lax.optimization_barrier((near, far, small))
    small = cross_sum(small, "y")
    near = [near[0], near[1], near[3], near[2]]
    far = [far[0], far[1], far[3], far[2]]
    whole = pl.BlockSpec(memory_space=pltpu.VMEM)
    square = pl.pallas_call(
        gather_kernel,
        in_specs=[pl.BlockSpec(memory_space=pltpu.SMEM)]
        + [pl.BlockSpec(memory_space=pl.ANY)] * (2 * sides),
        out_specs=whole,
        out_shape=jax.ShapeDtypeStruct((sides, 2 * sides * tok_rows, width), bf16),
        scratch_shapes=[pltpu.SemaphoreType.DMA((2 * sides * sides,))],
        compiler_params=params(0, 16),
        name="gather_square",
    )(jnp.stack([y, z, core]).astype(jnp.int32), *near, *far)
    return square, small


def context_kernel(wanted, place_ref, square_ref, band_ref, *out_refs):
    sides, tokens, _ = square_ref.shape
    half = tokens // 2
    for blocks, out_ref in zip(wanted, out_refs):
        for at, (step, part) in enumerate(blocks):
            block = lax.rem(place_ref[0] + step, sides)
            rows = square_ref[pl.ds(block, 1), part * half : (part + 1) * half, :][0]
            out_ref[at * half : (at + 1) * half, :] = jnp.dot(
                rows, band_ref[...], preferred_element_type=f32
            ).astype(bf16)


def weight_kernel(wanted, place_ref, square_ref, band_ref, *out_refs):
    sides, tokens, depth = square_ref.shape
    half = depth // sides // 2
    for blocks, out_ref in zip(wanted, out_refs):
        for at, (step, part) in enumerate(blocks):
            block = lax.rem(place_ref[0] + step, sides)
            columns = pl.ds(pl.multiple_of((2 * block + part) * half, half), half)
            out_ref[at * half : (at + 1) * half, :] = lax.dot_general(
                square_ref[:, :, columns].reshape(sides * tokens, half),
                band_ref[...],
                OVER_ROWS,
                preferred_element_type=f32,
            ).astype(bf16)


def projection(kernel, name, place, square, band, wanted):
    width = band.shape[1]
    half = square.shape[1] // 2
    count = sum(len(blocks) for blocks in wanted)
    whole = pl.BlockSpec(memory_space=pltpu.VMEM)
    return pl.pallas_call(
        functools.partial(kernel, wanted),
        in_specs=[pl.BlockSpec(memory_space=pltpu.SMEM), whole, whole],
        out_specs=tuple(whole for _ in wanted),
        out_shape=tuple(
            jax.ShapeDtypeStruct((half * len(blocks), width), bf16) for blocks in wanted
        ),
        compiler_params=params(0, 16),
        cost_estimate=pl.CostEstimate(
            flops=2 * half * count * band.shape[0] * width,
            bytes_accessed=5_000_000,
            transcendentals=0,
        ),
        name=name,
    )(place, square, *kept(band))


def kept(*arrays):
    return [pltpu.with_memory_space_constraint(a, pltpu.VMEM) for a in arrays]


def outside(*arrays):
    return [pltpu.with_memory_space_constraint(a, pltpu.HBM) for a in arrays]


def params(grid=0, mib=16):
    return pltpu.CompilerParams(
        vmem_limit_bytes=mib * MIB,
        dimension_semantics=("arbitrary",) * grid if grid else None,
    )


def slot_codes(routes_wide, experts, pieces, tok_rows):
    columns = pieces * tok_rows
    expert = lax.broadcasted_iota(jnp.int32, (experts, columns), 0)
    named = expert == routes_wide[0:1, :]
    for choice in range(1, routes_wide.shape[0]):
        named = named | (expert == routes_wide[choice : choice + 1, :])
    before = lax.broadcasted_iota(jnp.int32, (columns, columns), 0)
    after = lax.broadcasted_iota(jnp.int32, (columns, columns), 1)
    earlier = (before // tok_rows == after // tok_rows) & (before < after)
    rank = jnp.dot(
        jnp.where(named, 1.0, 0.0).astype(bf16),
        jnp.where(earlier, 1.0, 0.0).astype(bf16),
        preferred_element_type=f32,
    )
    piece = (lax.broadcasted_iota(jnp.int32, (experts, columns), 1) // tok_rows).astype(f32)
    return jnp.where(named, piece * 8.0 + rank, -1.0)


def row_codes(shape, capacity, block, dim):
    row = lax.broadcasted_iota(jnp.int32, shape, dim) % block
    return ((row // capacity) * 8 + row % capacity).astype(f32)


def place_kernel(
    capacity, pre_ref, grad_ref, gain_ref, routes_ref, send_ref, code_ref, normed_ref, source
):
    tok_rows, features = pre_ref.shape
    experts, columns = code_ref.shape
    pieces = features // WIDE
    block = pieces * capacity
    group = pl.program_id(0)
    some = send_ref.shape[0]
    rows = some * block

    @pl.when(group == 0)
    def prepare():
        hidden = pre_ref[...].astype(f32)
        inverse = lax.rsqrt(jnp.mean(hidden * hidden, axis=-1, keepdims=True) + 1e-06)
        normed = (hidden * inverse * gain_ref[...]).astype(bf16)
        normed_ref[...] = normed
        for piece in range(pieces):
            at = pl.ds(piece * tok_rows, tok_rows)
            source[at, :WIDE] = normed[:, piece * WIDE : (piece + 1) * WIDE]
            source[at, WIDE:] = grad_ref[:, piece * WIDE : (piece + 1) * WIDE]
        code_ref[...] = slot_codes(routes_ref[...], experts, pieces, tok_rows)

    code = code_ref[pl.ds(pl.multiple_of(group * some, some), some), :]
    want = row_codes((some, block, columns), capacity, block, 1)
    hit = jnp.where(code[:, None, :] == want, 1.0, 0.0).astype(bf16).reshape(rows, columns)
    moved = jnp.dot(hit, source[...], preferred_element_type=f32).astype(bf16)
    send_ref[:, :block, :] = moved[:, :WIDE].reshape(some, block, WIDE)
    send_ref[:, block:, :] = moved[:, WIDE:].reshape(some, block, WIDE)


def place(pre_norm, out_grad, norm_gain, routes_wide, experts, capacity):
    tok_rows, features = pre_norm.shape
    pieces = features // WIDE
    block = pieces * capacity
    some = 8
    columns = pieces * tok_rows

    def whole(*shape):
        return pl.BlockSpec(shape, lambda i: (0,) * len(shape))

    return pl.pallas_call(
        functools.partial(place_kernel, capacity),
        grid=(experts // some,),
        in_specs=[
            whole(tok_rows, features),
            whole(tok_rows, features),
            whole(1, features),
            whole(*routes_wide.shape),
        ],
        out_specs=(
            pl.BlockSpec((some, 2 * block, WIDE), lambda i: (i, 0, 0)),
            whole(experts, columns),
            whole(tok_rows, features),
        ),
        out_shape=(
            pltpu.HBM((experts, 2 * block, WIDE), bf16),
            jax.ShapeDtypeStruct((experts, columns), f32),
            jax.ShapeDtypeStruct((tok_rows, features), bf16),
        ),
        scratch_shapes=[pltpu.VMEM((columns, 2 * WIDE), bf16)],
        compiler_params=params(1, 16),
        name="place",
    )(*outside(pre_norm, out_grad, norm_gain), routes_wide)


def order_matrix(capacity, block):
    at = np.arange(SOME * block)
    moved = (at % block) // capacity * (SOME * capacity) + at // block * capacity + at % capacity
    return jnp.asarray(moved[None, :] == at[:, None], bf16)


def spread_kernel(capacity, got_ref, order_ref, rows_ref):
    some, block, _ = got_ref.shape
    pieces = block // capacity
    span = SOME * capacity
    for group in range(some // SOME):
        source = got_ref[group * SOME : (group + 1) * SOME].reshape(SOME * block, WIDE)
        moved = jnp.dot(order_ref[...], source, preferred_element_type=f32).astype(bf16)
        for piece in range(pieces):
            rows_ref[group * span : (group + 1) * span, piece * WIDE : (piece + 1) * WIDE] = moved[
                piece * span : (piece + 1) * span
            ]


def spread(got, kind, order, capacity):
    sources, double, _ = got.shape
    block = double // 2
    features = block // capacity * WIDE
    some = 2 * SOME
    return pl.pallas_call(
        functools.partial(spread_kernel, capacity),
        grid=(sources // some,),
        in_specs=[
            pl.BlockSpec((some, block, WIDE), lambda i: (i, kind, 0)),
            pl.BlockSpec(order.shape, lambda i: (0, 0)),
        ],
        out_specs=pl.BlockSpec((some * capacity, features), lambda i: (i, 0)),
        out_shape=jax.ShapeDtypeStruct((sources * capacity, features), bf16),
        compiler_params=params(1),
        name="spread",
    )(got, order)


def forward_kernel(own_ref, other_ref, gate_ref, up_ref, gate_pre_ref, up_pre_ref):
    count = own_ref.shape[0]
    units = gate_ref.shape[2]
    tile = 256
    for mat, out in ((gate_ref, gate_pre_ref), (up_ref, up_pre_ref)):
        for n in range(units // tile):
            at = slice(n * tile, (n + 1) * tile)
            out[:count, at] = jnp.dot(own_ref[...], mat[0, :, at], preferred_element_type=f32)
            out[count:, at] = jnp.dot(other_ref[...], mat[0, :, at], preferred_element_type=f32)


def forward(own, other, w_gate, w_up):
    count, features = own.shape
    units = w_gate.shape[2]
    inside = pl.BlockSpec(memory_space=pltpu.VMEM)
    return pl.pallas_call(
        forward_kernel,
        in_specs=[inside] * 4,
        out_specs=(inside, inside),
        out_shape=(jax.ShapeDtypeStruct((2 * count, units), f32),) * 2,
        compiler_params=params(0, 10),
        cost_estimate=pl.CostEstimate(
            flops=8 * count * features * units, bytes_accessed=24_000_000, transcendentals=0
        ),
        name="forward",
    )(own, other, *kept(w_gate, w_up))


def hidden_kernel(
    capacity, own_ref, other_ref, down_ref, gate_pre_ref, up_pre_ref, gg_ref, gu_ref, *part_refs
):
    count = own_ref.shape[0]
    units = down_ref.shape[1]
    tile = 256
    for half, rows in enumerate((own_ref, other_ref)):
        here = slice(half * count, (half + 1) * count)
        part = jnp.zeros((count, 1), f32)
        for n in range(units // tile):
            at = slice(n * tile, (n + 1) * tile)
            upstream = lax.dot_general(
                rows[...], down_ref[0, at, :], OVER_LAST, preferred_element_type=f32
            )
            gate_pre = gate_pre_ref[here, at]
            up_pre = up_pre_ref[here, at]
            sig = jax.nn.sigmoid(gate_pre)
            grad_up = upstream * (gate_pre * sig)
            part = part + jnp.sum(grad_up * up_pre, axis=-1, keepdims=True)
            gu_ref[here, at] = grad_up.astype(bf16)
            gg_ref[here, at] = (
                upstream * up_pre * sig * (1.0 + gate_pre * (1.0 - sig))
            ).astype(bf16)
        part_rows = part_refs[half].shape[0]
        rows_of = lax.broadcasted_iota(jnp.int32, (part_rows, count), 0)
        slots_of = lax.broadcasted_iota(jnp.int32, (part_rows, count), 1)
        same = (rows_of // 8 == slots_of // capacity) & (rows_of % 8 == slots_of % capacity)
        part_refs[half][...] = jnp.dot(
            jnp.where(same, 1.0, 0.0).astype(bf16),
            jnp.broadcast_to(part.astype(bf16), (count, 128)),
            preferred_element_type=f32,
        )


def hidden_grads(own, other, w_down, gate_pre, up_pre, capacity):
    count, features = own.shape
    units = w_down.shape[1]
    inside = pl.BlockSpec(memory_space=pltpu.VMEM)
    return pl.pallas_call(
        functools.partial(hidden_kernel, capacity),
        in_specs=[inside] * 5,
        out_specs=(inside,) * 4,
        out_shape=(
            jax.ShapeDtypeStruct((2 * count, units), bf16),
            jax.ShapeDtypeStruct((2 * count, units), bf16),
            jax.ShapeDtypeStruct((count // capacity * 8, 128), f32),
            jax.ShapeDtypeStruct((count // capacity * 8, 128), f32),
        ),
        compiler_params=params(0, 10),
        cost_estimate=pl.CostEstimate(
            flops=4 * count * features * units, bytes_accessed=24_000_000, transcendentals=0
        ),
        name="hidden_grads",
    )(*outside(own, other), *kept(w_down), gate_pre, up_pre)


def term_kernel(gg_ref, gu_ref, gate_ref, up_ref, own_ref, other_ref):
    count, features = own_ref.shape
    tile = 512
    for n in range(features // tile):
        at = slice(n * tile, (n + 1) * tile)
        term = lax.dot_general(
            gg_ref[...], gate_ref[0, at, :], OVER_LAST, preferred_element_type=f32
        )
        term = term + lax.dot_general(
            gu_ref[...], up_ref[0, at, :], OVER_LAST, preferred_element_type=f32
        )
        term = term.astype(bf16)
        own_ref[:, at] = term[:count]
        other_ref[:, at] = term[count:]


def terms(grad_gate, grad_up, w_gate, w_up):
    count = grad_gate.shape[0] // 2
    units = grad_gate.shape[1]
    features = w_gate.shape[1]
    inside = pl.BlockSpec(memory_space=pltpu.VMEM)
    return pl.pallas_call(
        term_kernel,
        in_specs=[inside] * 4,
        out_specs=(inside, inside),
        out_shape=(jax.ShapeDtypeStruct((count, features), bf16),) * 2,
        compiler_params=params(0, 10),
        cost_estimate=pl.CostEstimate(
            flops=8 * count * features * units, bytes_accessed=17_000_000, transcendentals=0
        ),
        name="terms",
    )(grad_gate, grad_up, *kept(w_gate, w_up))


def pack_kernel(
    capacity, own_ref, other_ref, order_ref, own_part_ref, other_part_ref, chip_ref, send_ref, held
):
    rows, features = own_ref.shape
    pieces = features // WIDE
    span = SOME * capacity
    block = pieces * capacity
    for group in range(rows // span):
        here = slice(group * span, (group + 1) * span)
        for piece in range(pieces):
            at = slice(piece * WIDE, (piece + 1) * WIDE)
            held[group, pl.ds(piece * span, span), :] = (
                own_ref[here, at].astype(f32) + other_ref[here, at].astype(f32)
            ).astype(bf16)
        moved = lax.dot_general(
            order_ref[...], held[group], OVER_ROWS, preferred_element_type=f32
        )
        send_ref[group * SOME : (group + 1) * SOME, :block, :] = moved.astype(bf16).reshape(
            SOME, block, WIDE
        )
    part = own_part_ref[...] + other_part_ref[...]
    high = part.astype(bf16).astype(f32)
    lane = lax.broadcasted_iota(jnp.int32, part.shape, 1)
    half = part.shape[1] // 2
    part = jnp.where(lane < half, high, part - high)
    part = jnp.where(lane % half == chip_ref[0], part, 0.0)
    part = part.reshape(send_ref.shape[0], 8, part.shape[1])
    part = jnp.concatenate(
        [part, jnp.zeros((*part.shape[:2], WIDE - part.shape[2]), f32)], axis=2
    )
    send_ref[:, block:, :] = part.astype(bf16)


def pack(own, other, order, capacity, own_part, other_part):
    count, features = own.shape
    block = features // WIDE * capacity
    groups = 2
    span = groups * SOME * capacity
    chip = lax.axis_index(CHIP).astype(jnp.int32).reshape(1)
    return pl.pallas_call(
        functools.partial(pack_kernel, capacity),
        grid=(count // span,),
        in_specs=[
            pl.BlockSpec((span, features), lambda i: (i, 0)),
            pl.BlockSpec((span, features), lambda i: (i, 0)),
            pl.BlockSpec(order.shape, lambda i: (0, 0)),
            pl.BlockSpec((groups * SOME * 8, 128), lambda i: (i, 0)),
            pl.BlockSpec((groups * SOME * 8, 128), lambda i: (i, 0)),
            pl.BlockSpec(memory_space=pltpu.SMEM),
        ],
        out_specs=pl.BlockSpec((groups * SOME, block + 8, WIDE), lambda i: (i, 0, 0)),
        out_shape=pltpu.HBM((count // capacity, block + 8, WIDE), bf16),
        scratch_shapes=[pltpu.VMEM((groups, SOME * block, WIDE), bf16)],
        compiler_params=params(1),
        name="pack",
    )(own, other, order, own_part, other_part, chip)


def mix_kernel(capacity, code_ref, gate_ref, mix_ref):
    some, columns = code_ref.shape
    rows = mix_ref.shape[1]
    block = rows // some
    want = row_codes((some, block, columns), capacity, block, 1)
    mixing = jnp.where(code_ref[...][:, None, :] == want, gate_ref[...][:, None, :], 0.0)
    mixing = mixing.reshape(rows, columns)
    high = mixing.astype(bf16)
    low = (mixing - high.astype(f32)).astype(bf16)
    mix_ref[:columns, :] = high.T
    mix_ref[columns:, :] = low.T


def mixings(code, gate_wide, capacity, block):
    experts, columns = code.shape
    some = 8
    return pl.pallas_call(
        functools.partial(mix_kernel, capacity),
        grid=(experts // some,),
        in_specs=[
            pl.BlockSpec((some, columns), lambda i: (i, 0)),
            pl.BlockSpec((some, columns), lambda i: (i, 0)),
        ],
        out_specs=pl.BlockSpec((2 * columns, some * block), lambda i: (0, i)),
        out_shape=jax.ShapeDtypeStruct((2 * columns, experts * block), bf16),
        compiler_params=params(1),
        name="mixings",
    )(code, gate_wide)


def finish_kernel(
    mix_ref, back_ref, pre_ref, grad_ref, gain_ref, router_ref, normed_ref,
    code_ref, gate_ref, routes_ref,
    residual_ref, bands_ref, small_ref, gate_grad_ref,
):
    tok_rows, features = pre_ref.shape
    columns = mix_ref.shape[0] // 2
    pieces = features // WIDE
    experts, rows, _ = back_ref.shape
    block = rows - 8
    both = jnp.dot(
        mix_ref[...],
        back_ref[:, :block, :].reshape(experts * block, WIDE),
        preferred_element_type=f32,
    )
    slot = lax.broadcasted_iota(jnp.int32, (experts, 8, tok_rows), 1).astype(f32)
    hit = jnp.where(code_ref[:, :tok_rows][:, None, :] == slot, 1.0, 0.0)
    part = back_ref[:, block:, :128].astype(f32).reshape(experts * 8, 128).astype(bf16)
    part = lax.dot_general(
        hit.reshape(experts * 8, tok_rows).astype(bf16), part, OVER_ROWS,
        preferred_element_type=f32,
    )
    grad_of = part[:, :experts] + part[:, experts:]
    expert = lax.broadcasted_iota(jnp.int32, (tok_rows, experts), 1)
    for choice in range(routes_ref.shape[1]):
        named = expert == routes_ref[:, choice : choice + 1]
        gate_grad_ref[:, choice : choice + 1] = jnp.sum(
            jnp.where(named, grad_of, 0.0), axis=-1, keepdims=True
        )
    gate_of = gate_ref[...]
    weighted = jnp.sum(gate_of * grad_of, axis=-1, keepdims=True)
    logit_full = (gate_of * (grad_of - weighted)).astype(bf16)
    expert_grad = both[:columns] + both[columns:]
    hidden = pre_ref[...].astype(f32)
    inverse = lax.rsqrt(jnp.mean(hidden * hidden, axis=-1, keepdims=True) + 1e-06)
    router_term = jnp.dot(logit_full, router_ref[...], preferred_element_type=f32)
    router_part = lax.dot_general(
        logit_full, normed_ref[...], OVER_ROWS, preferred_element_type=f32
    )
    spare = small_ref.shape[1] - experts
    per_band = bands_ref.shape[2] // WIDE
    moment = jnp.zeros((tok_rows, 1), f32)
    normed_grads = []
    for piece in range(pieces):
        at = slice(piece * WIDE, (piece + 1) * WIDE)
        normed_grad = (
            expert_grad[piece * tok_rows : (piece + 1) * tok_rows] + router_term[:, at]
        )
        normed_grads.append(normed_grad)
        small_ref[piece, :experts, :] = router_part[:, at]
        small_ref[piece, experts:, :] = jnp.broadcast_to(
            jnp.sum(normed_grad * hidden[:, at] * inverse, axis=0, keepdims=True), (spare, WIDE)
        )
        moment = moment + jnp.sum(
            hidden[:, at] * gain_ref[:, at] * normed_grad, axis=-1, keepdims=True
        )
    factor = inverse * inverse * inverse * (moment / features)
    for piece in range(pieces):
        at = slice(piece * WIDE, (piece + 1) * WIDE)
        residual = (
            grad_ref[:, at].astype(f32)
            + inverse * gain_ref[:, at] * normed_grads[piece]
            - hidden[:, at] * factor
        ).astype(bf16)
        residual_ref[:, at] = residual
        inner = piece % per_band * WIDE
        bands_ref[piece // per_band, :, inner : inner + WIDE] = residual


def finish(
    mix, back, pre_norm, out_grad, norm_gain, router_wide, normed, code, gate_of, routes, bands
):
    tok_rows, features = pre_norm.shape
    experts = gate_of.shape[1]
    return pl.pallas_call(
        finish_kernel,
        out_shape=(
            jax.ShapeDtypeStruct((tok_rows, features), bf16),
            jax.ShapeDtypeStruct((bands, tok_rows, features // bands), bf16),
            jax.ShapeDtypeStruct((features // WIDE, experts + 8, WIDE), f32),
            jax.ShapeDtypeStruct(routes.shape, f32),
        ),
        compiler_params=params(0, 24),
        name="finish",
    )(
        mix,
        *outside(back, pre_norm, out_grad, norm_gain),
        router_wide,
        *outside(normed),
        code,
        gate_of,
        routes,
    )


def shards(
    pre_norm,
    out_grad,
    routes,
    gate_probs,
    norm_gain,
    router_weight,
    w_gate,
    w_up,
    w_down,
    context,
    out_weight,
):
    tok_rows, features = pre_norm.shape
    top = routes.shape[1]
    experts = router_weight.shape[1]
    capacity = tok_rows * top * 3 // (2 * experts)
    pieces = features // WIDE
    block = pieces * capacity
    gain = norm_gain.reshape(1, features)

    routes_wide = jnp.tile(routes.T, (1, pieces))
    send, code, normed = place(pre_norm, out_grad, gain, routes_wide, experts, capacity)

    got = exchange(send, CHIP)

    order = order_matrix(capacity, block)
    got, code, normed, out_weight, context, routes, gate_probs = lax.optimization_barrier(
        (got, code, normed, out_weight, context, routes, gate_probs)
    )

    weight_band = lax.all_gather(out_weight, "x", axis=0, tiled=True)
    context_band = lax.all_gather(context, "y", axis=0, tiled=True)

    own_tokens = spread(got, 0, order, capacity)
    other_tokens = swap_cores(own_tokens)
    own_grads = spread(got, 1, order, capacity)
    other_grads = swap_cores(own_grads)
    gate_pre, up_pre = forward(own_tokens, other_tokens, w_gate, w_up)
    grad_gate, grad_up, own_part, other_part = hidden_grads(
        own_grads, other_grads, w_down, gate_pre, up_pre, capacity
    )
    other_part = swap_cores(other_part)
    own_term, other_term = terms(grad_gate, grad_up, w_gate, w_up)
    other_term = swap_cores(other_term)
    other_term, weight_band, context_band = lax.optimization_barrier(
        (other_term, weight_band, context_band)
    )
    send_back = pack(own_term, other_term, order, capacity, own_part, other_part)
    send_back, code, routes, gate_probs, router_weight = lax.optimization_barrier(
        (send_back, code, routes, gate_probs, router_weight)
    )
    got_back = exchange(send_back, CHIP)

    named = routes[:, :, None] == jnp.arange(experts, dtype=jnp.int32)[None, None, :]
    gate_of = jnp.sum(jnp.where(named, gate_probs[:, :, None], 0.0), axis=1)
    mix = mixings(code, jnp.tile(gate_of.T, (1, pieces)), capacity, block)
    router_wide = router_weight.T

    got_back, mix, router_wide, gate_of = lax.optimization_barrier(
        (got_back, mix, router_wide, gate_of)
    )
    residual_grad, bands, small, gate_grad = finish(
        mix, got_back, pre_norm, out_grad, gain, router_wide, normed, code, gate_of, routes,
        lax.axis_size("y"),
    )

    square, small = gather_square(bands, small)
    context_grad, weight_grad, small = ring_scatter(
        square,
        (
            (functools.partial(projection, context_kernel, "context_part"), weight_band, "y"),
            (functools.partial(projection, weight_kernel, "weight_part"), context_band, "x"),
        ),
        small,
    )
    router_grad = small[:experts].T
    gain_grad = small[experts]
    return (residual_grad, gate_grad, router_grad, gain_grad, context_grad, weight_grad)


def solution(mesh):
    devices = np.asarray(mesh.devices)
    fine = Mesh(devices.reshape(4, 4, 4, 2), EVERY)
    rows = P(EVERY, None)
    cube = P(EVERY, None, None)
    split = P(DP, TENSOR)
    return jax.shard_map(
        shards,
        mesh=fine,
        in_specs=(rows, rows, rows, rows, P(), P(), cube, cube, cube, split, split),
        out_specs=(rows, rows, P(TENSOR, None), P(TENSOR), split, split),
        check_vma=False,
    )
```
